32 devices in a mesh: replica: 4 (over x, core), expert: 8 (over z, y).
Axes of the slice: x: 2, y: 2, z: 4, core: 2. Of those that a mesh axis runs over, the one named last changes fastest.
Arguments:
- tokens: bfloat16 [4, 1024, 4096], P('replica', 'expert'), may hold values from -4 to 4
- routes: int32 [4, 1024, 8], P('replica', 'expert'), may hold values from 0 to 127, as said below
- cweights: float32 [4, 1024, 8], P('replica', 'expert'), may hold values from 0.1 to 1
- w_gate: bfloat16 [4, 4096, 1024], P('replica', None, 'expert'), may hold values from -0.09375 to 0.09375
- w_up: bfloat16 [4, 4096, 1024], P('replica', None, 'expert'), may hold values from -0.09375 to 0.09375
- w_down: bfloat16 [4, 1024, 4096], P('replica', 'expert'), may hold values from -0.1875 to 0.1875
- grad_out: bfloat16 [4, 1024, 4096], P('replica', 'expert'), may hold values from -4 to 4
- frag_local: bfloat16 [4, 2, 1024, 4096], P('replica', None, 'expert'), may hold values from -2000 to 2000
- frag_global: float32 [2, 1024, 4096], P(None, 'expert', 'replica'), may hold values from -2 to 2
- frag_moment: float32 [2, 1024, 4096], P(None, 'expert', 'replica'), may hold values from -4 to 4
Outputs:
- layer_out: bfloat16 [4, 1024, 4096], P('replica', 'expert')
- grad_tokens: bfloat16 [4, 1024, 4096], P('replica', 'expert')
- grad_gate: bfloat16 [4, 4096, 1024], P('replica', None, 'expert')
- grad_up: bfloat16 [4, 4096, 1024], P('replica', None, 'expert')
- grad_down: bfloat16 [4, 1024, 4096], P('replica', 'expert')
- new_global: float32 [2, 1024, 4096], P(None, 'expert', 'replica')
- new_moment: float32 [2, 1024, 4096], P(None, 'expert', 'replica')
- new_local: bfloat16 [4, 2, 1024, 4096], P('replica', None, 'expert')
The draws below stay inside these ranges and needn't reach their ends.
Inputs may be any that keep to these rules, and one draw needn't show every extreme that they name: `routes`: ids in a row are distinct. In each block of 128 rows of one device, each id below 1 is named by at most 32 rows; in every draw one id below 1 is named by exactly 32 rows in every block.
All inputs are finite; a program needn't handle non-finite values.
Results may differ from the reference program's by a relative error of at most 0.009.
Values may be sent and summed in bfloat16 or wider, within the bound.
A program may use at most 128 MiB of HBM per device.

```python
import math
import jax
import jax.numpy as jnp
from jax import lax

D = 4096
HID = 1024
EXPERTS_ALL = 128
TOP = 8
EXP_WIN = 1
TOK_DEV = 128
CAP = 32
TOK_REP = 1024
REPLICAS = 4
FRAG_EXP = 2


def frag_scales(key):
    key_rows, key_cols, key_anchor, key_row_blocks, key_col_blocks = jax.random.split(key, 5)
    row_scale = jnp.exp(jax.random.uniform(key_rows, (FRAG_EXP, HID, 1)) * math.log(3.2))
    row_scale = row_scale * (0.5 + jnp.arange(HID, dtype=jnp.float32)[None, :, None] / HID)
    row_blocks = jnp.exp(jax.random.uniform(key_row_blocks, (FRAG_EXP, 8, 1), minval=-1.0, maxval=1.0) * math.log(2.0))
    row_scale = row_scale * jnp.repeat(row_blocks, HID // 8, axis=1)
    col_scale = jnp.exp(jax.random.uniform(key_cols, (1, 1, D)) * math.log(3.2))
    col_scale = col_scale * (0.5 + jnp.arange(D, dtype=jnp.float32)[None, None, :] / D)
    col_blocks = jnp.exp(jax.random.uniform(key_col_blocks, (1, 1, 4), minval=-1.0, maxval=1.0) * math.log(2.0))
    col_scale = col_scale * jnp.repeat(col_blocks, D // 4, axis=2)
    scales = row_scale * col_scale
    anchor = jax.random.truncated_normal(key_anchor, -4.0, 4.0, (FRAG_EXP, HID, D)) * 0.5
    return (scales, anchor)


def draw_frag_global(key, part):
    scales, anchor = frag_scales(key)
    return anchor.astype(jnp.float32)


def draw_frag_local(key, part):
    scales, anchor = frag_scales(key)
    key = jax.random.fold_in(key, 5)
    key_own = jax.random.fold_in(key, 1)
    key_pick = jax.random.fold_in(key, 2)
    key_replica_blocks = jax.random.fold_in(key, 3)
    own = jax.random.truncated_normal(key_own, -4.0, 4.0, (REPLICAS, FRAG_EXP, HID, D)) * math.sqrt(REPLICAS)
    replica_drift = jnp.exp(jax.random.uniform(key_replica_blocks, (REPLICAS, FRAG_EXP, 1, 4), minval=-1.0, maxval=1.0) * math.log(2.0))
    own = own * jnp.repeat(replica_drift, D // 4, axis=3)
    parity = jax.random.randint(key_pick, (), 0, 2)
    amplitude = jnp.where(jnp.arange(FRAG_EXP) % 2 == parity, 0.2, 0.6).astype(jnp.float32)
    amplitude = amplitude[None, :, None, None]
    offsets = own
    return (anchor[None] + scales[None] * amplitude * offsets).astype(jnp.bfloat16)


def draw_routes(key, part):
    key = jax.random.fold_in(key, 7)
    key_full, key_counts, key_orders, key_others, key_shuffle = jax.random.split(key, 5)
    blocks = REPLICAS * (TOK_REP // TOK_DEV)
    tokens_all = blocks * TOK_DEV
    fullest = jax.random.randint(key_full, (), 0, EXP_WIN)
    counts = jax.random.randint(key_counts, (blocks, EXP_WIN), 1, CAP + 1)
    counts = jnp.where(jnp.arange(EXP_WIN)[None, :] == fullest, CAP, counts)
    orders = jax.vmap(lambda subkey: jax.random.permutation(subkey, TOK_DEV))(jax.random.split(key_orders, blocks * EXP_WIN))
    rank_of = jnp.argsort(orders, axis=1).reshape(blocks, EXP_WIN, TOK_DEV)
    routed = (rank_of < counts[:, :, None]).astype(jnp.int32)
    routed = jnp.transpose(routed, (0, 2, 1)).reshape(tokens_all, EXP_WIN)
    others = jax.vmap(lambda subkey: jax.random.permutation(subkey, EXPERTS_ALL - EXP_WIN)[:TOP])(jax.random.split(key_others, tokens_all)) + EXP_WIN
    places = jnp.cumsum(routed, axis=1) - 1
    number = jnp.sum(routed, axis=1)
    slot_ids = jnp.arange(TOP)
    chosen = jnp.sum(jnp.where((routed[:, :, None] == 1) & (places[:, :, None] == slot_ids[None, None, :]), jnp.arange(EXP_WIN)[None, :, None], 0), axis=1)
    route_ids = jnp.where(slot_ids[None, :] < number[:, None], chosen, others)
    shuffle = jax.vmap(lambda subkey: jax.random.permutation(subkey, TOP))(jax.random.split(key_shuffle, tokens_all))
    route_ids = jnp.take_along_axis(route_ids, shuffle, axis=1)
    return route_ids.reshape(REPLICAS, TOK_REP, TOP).astype(jnp.int32)


def level_of(own_key, dims, cuts, low, largest):
    def one(dim, parts):
        heights = jax.random.uniform(jax.random.fold_in(jax.random.fold_in(own_key, 6), dim), (parts,), jnp.float32, low / len(cuts), largest / len(cuts))
        return jnp.repeat(jnp.exp(heights), dims[dim] // parts).reshape((-1,) + (1,) * (len(dims) - dim - 1))

    level = one(*cuts[0])
    for cut in cuts[1:]:
        level = level * one(*cut)
    return level


def noise(rng, dims, width, reach, cuts=(), held_as=jnp.bfloat16):
    result = width * jax.random.normal(rng, dims, jnp.float32)
    if cuts:
        result = result * level_of(rng, dims, cuts, -0.22, 0.18)
    return jnp.clip(result, -reach, reach).astype(held_as)


def setup_inputs(seed: int = 0) -> dict:
    key_list = jax.random.split(jax.random.key(seed), 11)
    return {
        "tokens": noise(key_list[0], (REPLICAS, TOK_REP, D), 1.0, 4.0, ((0, 4), (1, 8))),
        "routes": draw_routes(jax.random.fold_in(key_list[10], 71), 0),
        "cweights": jnp.clip(0.1 + 0.9 * jax.random.uniform(key_list[2], (REPLICAS, TOK_REP, TOP), jnp.float32) ** level_of(key_list[2], (REPLICAS, TOK_REP, TOP), ((0, 4), (1, 8)), -0.2, 0.2), 0.1, 1.0),
        "w_gate": noise(key_list[3], (REPLICAS, D, EXP_WIN * HID), D ** -0.5, 0.09375, ((0, 4), (2, 8))),
        "w_up": noise(key_list[4], (REPLICAS, D, EXP_WIN * HID), D ** -0.5, 0.09375, ((0, 4), (2, 8))),
        "w_down": noise(key_list[5], (REPLICAS, EXP_WIN * HID, D), HID ** -0.5, 0.1875, ((0, 4), (1, 8))),
        "grad_out": noise(key_list[6], (REPLICAS, TOK_REP, D), 1.0, 4.0, ((0, 4), (1, 8))),
        "frag_local": draw_frag_local(jax.random.fold_in(key_list[10], 71), 0),
        "frag_global": draw_frag_global(jax.random.fold_in(key_list[10], 71), 0),
        "frag_moment": noise(key_list[9], (FRAG_EXP, HID, D), 0.3, 4.0, ((1, 8), (2, 4)), jnp.float32),
    }


def silu_parts(gate_pre):
    sigmoid_val = jax.nn.sigmoid(gate_pre)
    return (gate_pre * sigmoid_val, sigmoid_val * (1.0 + gate_pre * (1.0 - sigmoid_val)))

def one_replica(operands):
    inputs, route_ids, weights, wg_all, wu_all, wd_all, grads_in = operands
    blocks = TOK_REP // TOK_DEV
    precise = lax.Precision.HIGHEST
    experts = jnp.arange(EXP_WIN, dtype=jnp.int32)
    matched = route_ids[:, :, None] == experts[None, None, :]
    routed = jnp.any(matched, axis=1).astype(jnp.int32).reshape(blocks, TOK_DEV, EXP_WIN)
    shares = lax.optimization_barrier(jnp.sum(jnp.where(matched, weights[:, :, None], jnp.float32(0.0)), axis=1)).reshape(blocks, TOK_DEV, EXP_WIN)
    places = jnp.cumsum(routed, axis=1) - 1
    slot_ids = jnp.arange(CAP, dtype=jnp.int32)
    layout = ((routed[:, None] == 1) & (places[:, None] == slot_ids[None, :, None, None])).astype(jnp.float32)
    tok_f32 = inputs.astype(jnp.float32).reshape(blocks, TOK_DEV, D)
    grad_f32 = grads_in.astype(jnp.float32).reshape(blocks, TOK_DEV, D)
    picked = jnp.einsum('bcte,btd->ebcd', layout, tok_f32, precision=precise).astype(jnp.bfloat16)
    slot_share = jnp.einsum('bcte,bte->ebc', layout, shares, precision=precise)
    dy_rows = (jnp.einsum('bcte,btd->ebcd', layout, grad_f32, precision=precise) * slot_share[..., None]).astype(jnp.bfloat16)
    layer_sum = jnp.zeros((blocks, TOK_DEV, D), jnp.float32)
    grad_sum = jnp.zeros((blocks, TOK_DEV, D), jnp.float32)
    grad_gates, grad_ups, grad_downs = ([], [], [])
    for expert in range(EXP_WIN):
        wg_e = wg_all[:, expert * HID:(expert + 1) * HID]
        wu_e = wu_all[:, expert * HID:(expert + 1) * HID]
        wd_e = wd_all[expert * HID:(expert + 1) * HID, :]
        tok_rows = picked[expert].reshape(blocks * CAP, D)
        grad_rows = dy_rows[expert].reshape(blocks * CAP, D)
        gate_pre = jnp.dot(tok_rows, wg_e, preferred_element_type=jnp.float32)
        up_pre = jnp.dot(tok_rows, wu_e, preferred_element_type=jnp.float32)
        silu_val, silu_slope = silu_parts(gate_pre)
        hidden_act = (silu_val * up_pre).astype(jnp.bfloat16)
        expert_out = jnp.dot(hidden_act, wd_e, preferred_element_type=jnp.float32).reshape(blocks, CAP, D)
        weighted = layout[..., expert] * shares[:, None, :, expert]
        layer_sum = layer_sum + jnp.einsum('bct,bcd->btd', weighted, expert_out, precision=precise)
        grad_hidden = jnp.dot(grad_rows, wd_e.T, preferred_element_type=jnp.float32)
        grad_gate_pre = (grad_hidden * up_pre * silu_slope).astype(jnp.bfloat16)
        grad_up_pre = (grad_hidden * silu_val).astype(jnp.bfloat16)
        grad_gates.append(jnp.dot(tok_rows.T, grad_gate_pre, preferred_element_type=jnp.float32).astype(jnp.bfloat16))
        grad_ups.append(jnp.dot(tok_rows.T, grad_up_pre, preferred_element_type=jnp.float32).astype(jnp.bfloat16))
        grad_downs.append(jnp.dot(hidden_act.T, grad_rows, preferred_element_type=jnp.float32).astype(jnp.bfloat16))
        expert_dx = jnp.dot(grad_gate_pre, wg_e.T, preferred_element_type=jnp.float32) + jnp.dot(grad_up_pre, wu_e.T, preferred_element_type=jnp.float32)
        grad_sum = grad_sum + jnp.einsum('bct,bcd->btd', layout[..., expert], expert_dx.reshape(blocks, CAP, D), precision=precise)
    return (layer_sum.reshape(TOK_REP, D).astype(jnp.bfloat16), grad_sum.reshape(TOK_REP, D).astype(jnp.bfloat16), jnp.concatenate(grad_gates, axis=1), jnp.concatenate(grad_ups, axis=1), jnp.concatenate(grad_downs, axis=0))

def reference(tokens, routes, cweights, w_gate, w_up, w_down, grad_out, frag_local, frag_global, frag_moment):
    layer_out, grad_tokens, grad_gate, grad_up, grad_down = lax.map(one_replica, (tokens, routes, cweights, w_gate, w_up, w_down, grad_out))
    summed = lax.optimization_barrier(jnp.sum(frag_local.astype(jnp.float32), axis=0))
    pseudo = frag_global - summed / REPLICAS
    squares = lax.optimization_barrier(jnp.sum(pseudo * pseudo, axis=(1, 2)))
    clip_limit = 0.5 * (HID * D) ** 0.5
    factor = jnp.minimum(jnp.float32(1.0), clip_limit / (jnp.sqrt(squares) + 1e-06))
    clipped = pseudo * factor[:, None, None]
    new_moment = 0.9 * frag_moment + clipped
    new_global = frag_global - 0.7 * (0.9 * new_moment + clipped)
    new_local = jnp.broadcast_to(new_global.astype(jnp.bfloat16)[None], (REPLICAS, FRAG_EXP, HID, D))
    return (layer_out, grad_tokens, grad_gate, grad_up, grad_down, new_global, new_moment, new_local)
```

```python
import functools

import jax
import jax.numpy as jnp
from jax import lax
from jax.experimental import pallas as pl
from jax.experimental.pallas import tpu as pltpu
from jax.sharding import PartitionSpec as P

D = 4096
HID = 1024
SPLIT = 8
CAP = 32


OUTER_MOMENTUM = 0.9
OUTER_RATE = 0.7
CLIP_RMS = 0.5


def silu_parts(gate_pre):
    sigmoid_val = jax.nn.sigmoid(gate_pre)
    return (gate_pre * sigmoid_val, sigmoid_val * (1.0 + gate_pre * (1.0 - sigmoid_val)))


def outer_update(pseudo, squares, moment, anchor):
    clip_limit = CLIP_RMS * (HID * D) ** 0.5
    factor = jnp.minimum(jnp.float32(1.0), clip_limit / (jnp.sqrt(squares) + 1e-06))
    clipped = pseudo * factor[:, None, None]
    moment_next = OUTER_MOMENTUM * moment + clipped
    anchor_next = anchor - OUTER_RATE * (OUTER_MOMENTUM * moment_next + clipped)
    return (moment_next, anchor_next)


def general_body(
    tokens, routes, cweights, w_gate, w_up, w_down, grad_out, frag_local, frag_global, frag_moment
):
    groups = lax.axis_size("expert")
    window = groups // SPLIT
    precise = lax.Precision.HIGHEST
    inputs = tokens[0]
    grads_in = grad_out[0]
    route_ids = routes[0]
    weights = cweights[0]
    wg_part = w_gate[0]
    wu_part = w_up[0]
    wd_part = w_down[0]
    model_width = inputs.shape[1]
    experts = jnp.arange(window, dtype=jnp.int32)
    matched = route_ids[:, :, None] == experts[None, None, :]
    routed = jnp.any(matched, axis=1).astype(jnp.int32)
    shares = jnp.sum(jnp.where(matched, weights[:, :, None], jnp.float32(0.0)), axis=1)
    places = jnp.cumsum(routed, axis=0) - 1
    slot_ids = jnp.arange(CAP, dtype=jnp.int32)
    layout = (routed.T[:, None, :] == 1) & (places.T[:, None, :] == slot_ids[None, :, None])
    layout_f = layout.astype(jnp.float32)
    layout_b = layout.astype(jnp.bfloat16)
    combine = layout_f * shares.T[:, None, :]
    slot_share = jnp.sum(combine, axis=2)
    picked = jnp.einsum("ect,td->ecd", layout_b, inputs, preferred_element_type=jnp.float32).astype(
        jnp.bfloat16
    )
    outbound = jnp.broadcast_to(picked[:, None], (window, SPLIT, CAP, model_width)).reshape(
        groups, CAP, model_width
    )
    received = lax.all_to_all(outbound, "expert", split_axis=0, concat_axis=0, tiled=True)
    n_source, n_rows, width_in = received.shape
    flat = received.reshape(n_source * n_rows, width_in)
    gate_pre = jnp.dot(flat, wg_part, preferred_element_type=jnp.float32)
    up_pre = jnp.dot(flat, wu_part, preferred_element_type=jnp.float32)
    silu_val, silu_slope = silu_parts(gate_pre)
    hidden_act = (silu_val * up_pre).astype(jnp.bfloat16)
    partial_value = jnp.dot(hidden_act, wd_part, preferred_element_type=jnp.float32)
    partial_out, hidden_act, gate_pre, up_pre, rows_in = (
        partial_value.reshape(n_source, n_rows, width_in),
        hidden_act.reshape(n_source, n_rows, -1),
        gate_pre.reshape(n_source, n_rows, -1),
        up_pre.reshape(n_source, n_rows, -1),
        received,
    )
    returned = lax.all_to_all(partial_out, "expert", split_axis=0, concat_axis=0, tiled=True)
    expert_out = jnp.sum(returned.reshape(window, SPLIT, CAP, model_width), axis=1)
    layer_out = jnp.einsum(
        "ect,ecd->td", combine, expert_out, precision=precise, preferred_element_type=jnp.float32
    ).astype(jnp.bfloat16)
    dy_picked = jnp.einsum("ect,td->ecd", layout_b, grads_in, preferred_element_type=jnp.float32)
    dy_scaled = (dy_picked * slot_share[:, :, None]).astype(jnp.bfloat16)
    outbound_dy = jnp.broadcast_to(dy_scaled[:, None], (window, SPLIT, CAP, model_width)).reshape(
        groups, CAP, model_width
    )
    rows_dy = lax.all_to_all(outbound_dy, "expert", split_axis=0, concat_axis=0, tiled=True)
    grad_rows = rows_dy.reshape(-1, model_width)
    tok_rows = rows_in.reshape(-1, model_width)
    act_rows = hidden_act.reshape(grad_rows.shape[0], -1)
    gate_rows = gate_pre.reshape(grad_rows.shape[0], -1)
    up_rows = up_pre.reshape(grad_rows.shape[0], -1)
    grad_hidden = jnp.einsum("rd,hd->rh", grad_rows, wd_part, preferred_element_type=jnp.float32)
    silu_val, silu_slope = silu_parts(gate_rows)
    grad_gate_pre = (grad_hidden * up_rows * silu_slope).astype(jnp.bfloat16)
    grad_up_pre = (grad_hidden * silu_val).astype(jnp.bfloat16)
    grad_gate = jnp.einsum(
        "rd,rh->dh", tok_rows, grad_gate_pre, preferred_element_type=jnp.float32
    ).astype(jnp.bfloat16)[None]
    grad_up = jnp.einsum(
        "rd,rh->dh", tok_rows, grad_up_pre, preferred_element_type=jnp.float32
    ).astype(jnp.bfloat16)[None]
    grad_down = jnp.einsum(
        "rh,rd->hd", act_rows, grad_rows, preferred_element_type=jnp.float32
    ).astype(jnp.bfloat16)[None]
    partial_dx = jnp.einsum(
        "rh,dh->rd", grad_gate_pre, wg_part, preferred_element_type=jnp.float32
    ) + jnp.einsum("rh,dh->rd", grad_up_pre, wu_part, preferred_element_type=jnp.float32)
    partial_dx = partial_dx.reshape(groups, CAP, model_width)
    returned_dx = lax.all_to_all(partial_dx, "expert", split_axis=0, concat_axis=0, tiled=True)
    expert_dx = jnp.sum(returned_dx.reshape(window, SPLIT, CAP, model_width), axis=1)
    grad_tokens = jnp.einsum(
        "ect,ecd->td", layout_f, expert_dx, precision=precise, preferred_element_type=jnp.float32
    ).astype(jnp.bfloat16)
    replicas = lax.axis_size("replica")
    local_terms = frag_local[0].astype(jnp.float32)
    summed = lax.psum_scatter(
        local_terms.astype(jnp.bfloat16), "replica", scatter_dimension=2, tiled=True
    ).astype(jnp.float32)
    pseudo = frag_global - summed / replicas
    squares = lax.psum(jnp.sum(pseudo * pseudo, axis=(1, 2)), ("replica", "expert"))
    new_moment, new_global = outer_update(pseudo, squares, frag_moment, frag_global)
    new_local = lax.all_gather(new_global.astype(jnp.bfloat16), "replica", axis=2, tiled=True)[None]
    return (
        layer_out[None],
        grad_tokens[None],
        grad_gate,
        grad_up,
        grad_down,
        new_global,
        new_moment,
        new_local,
    )


MESH = pl.DeviceIdType.MESH
INNER = 2
COLS = 512
NT = (((1,), (1,)), ((), ()))
TN = (((0,), (0,)), ((), ()))


def step_kernel(
    groups,
    replicas,
    x_ref,
    dy_ref,
    share_ref,
    wg_ref,
    wu_ref,
    wd_ref,
    fl_ref,
    fg_ref,
    fm_ref,
    rows_ref,
    dx_ref,
    gg_ref,
    gu_ref,
    gd_ref,
    ng_ref,
    nm_ref,
    nl_ref,
    xs,
    ys,
    part,
    part_dx,
    from_pair,
    from_left,
    from_right,
    wgu,
    wd,
    pre,
    hid,
    act_t,
    dpre,
    ggu,
    gdn,
    pieces,
    fg,
    fm,
    pseudo,
    fresh,
    sq_part,
    sq_exp,
    sq_rep,
    load_sem,
    store_sem,
    gather_send,
    gather_recv,
    gpair_send,
    gpair_recv,
    red_send,
    red_recv,
    rpair_send,
    rpair_recv,
    frag_send,
    frag_recv,
    frag_own_sem,
    sqe_send,
    sqe_recv,
    sqr_send,
    sqr_recv,
    new_send,
    new_recv,
    new_own_sem,
):
    rep = lax.axis_index("replica")
    me = lax.axis_index("expert")
    outer = groups // INNER
    z = me // INNER
    y = me % INNER
    pair = z * INNER + (1 - y)
    width = x_ref.shape[1]
    hidden = wd_ref.shape[0]
    share_cols = fg_ref.shape[2]
    frags = fg_ref.shape[0]
    frag_rows = fg_ref.shape[1]

    loads = [
        pltpu.make_async_copy(wg_ref, wgu.at[:, pl.ds(0, hidden)], load_sem.at[0]),
        pltpu.make_async_copy(wu_ref, wgu.at[:, pl.ds(hidden, hidden)], load_sem.at[1]),
        pltpu.make_async_copy(wd_ref, wd, load_sem.at[2]),
        pltpu.make_async_copy(fg_ref, fg, load_sem.at[3]),
        pltpu.make_async_copy(fm_ref, fm, load_sem.at[4]),
    ]
    for load in loads:
        load.start()

    barrier = pltpu.get_barrier_semaphore()
    for j in range(1, groups):
        pl.semaphore_signal(
            barrier, inc=1, device_id=(rep, lax.rem(me + j, groups)), device_id_type=MESH
        )
    for j in range(1, replicas):
        pl.semaphore_signal(
            barrier, inc=1, device_id=(lax.rem(rep + j, replicas), me), device_id_type=MESH
        )
    pl.semaphore_wait(barrier, groups - 1 + replicas - 1)

    def block(z_of, y_of):
        return pl.ds(pl.multiple_of((z_of * INNER + y_of) * CAP, CAP), CAP)

    def remote(src, dst, send, recv, target):
        return pltpu.make_async_remote_copy(
            src_ref=src,
            dst_ref=dst,
            send_sem=send,
            recv_sem=recv,
            device_id=target,
            device_id_type=MESH,
        )

    def right():
        return (rep, jnp.minimum(z + 1, outer - 1) * INNER + y)

    def left():
        return (rep, jnp.maximum(z - 1, 0) * INNER + y)

    def gather_copy(buf, which, way, hop, z_src):
        rows = buf.at[block(z_src, y)]
        return remote(
            rows,
            rows,
            gather_send.at[which, way, hop],
            gather_recv.at[which, way, hop],
            right() if way == 0 else left(),
        )

    def gather_pair(buf, which, z_src, y_src):
        rows = buf.at[block(z_src, y_src)]
        return remote(
            rows, rows, gpair_send.at[which, z_src], gpair_recv.at[which, z_src], (rep, pair)
        )

    def gather_step(buf, which, hop):
        if hop == 0:

            @pl.when(z < outer - 1)
            def _():
                gather_copy(buf, which, 0, 0, z).start()

            @pl.when(z > 0)
            def _():
                gather_copy(buf, which, 1, 0, z).start()

            gather_pair(buf, which, z, y).start()
            return

        @pl.when(z >= hop)
        def _():
            gather_copy(buf, which, 0, hop - 1, z - hop).wait_recv()

            if hop < outer - 1:

                @pl.when(z < outer - 1)
                def _():
                    gather_copy(buf, which, 0, hop, z - hop).start()

            gather_pair(buf, which, z - hop, y).start()

        @pl.when(z + hop < outer)
        def _():
            gather_copy(buf, which, 1, hop - 1, z + hop).wait_recv()

            if hop < outer - 1:

                @pl.when(z > 0)
                def _():
                    gather_copy(buf, which, 1, hop, z + hop).start()

            gather_pair(buf, which, z + hop, y).start()

    def gather_finish(buf, which):
        for z_src in range(outer):
            gather_pair(buf, which, z_src, 1 - y).wait_recv()

    def gather_drain(buf, which):
        for hop in range(outer - 1):

            @pl.when((z < outer - 1) & (z >= hop))
            def _():
                gather_copy(buf, which, 0, hop, z - hop).wait_send()

            @pl.when((z > 0) & (z + hop < outer))
            def _():
                gather_copy(buf, which, 1, hop, z + hop).wait_send()

        for z_src in range(outer):
            gather_pair(buf, which, z_src, y).wait_send()

    order = []
    for k in range(outer // 2):
        order += [outer - 1 - k, k]
    if outer % 2:
        order.append(outer // 2)

    def reduce_pair(buf, which, z_dst):
        return remote(
            buf.at[block(z_dst, 1 - y)],
            from_pair.at[which, z_dst],
            rpair_send.at[which, z_dst],
            rpair_recv.at[which, z_dst],
            (rep, pair),
        )

    def reduce_line(buf, which, way, z_dst):
        landing = from_left if way == 0 else from_right
        return remote(
            buf.at[block(z_dst, y)],
            landing.at[which, z_dst],
            red_send.at[which, way, z_dst],
            red_recv.at[which, way, z_dst],
            right() if way == 0 else left(),
        )

    def reduce_start(buf, which):
        for z_dst in order:
            reduce_pair(buf, which, z_dst).start()

    def add_in(buf, z_dst, landed):
        rows = block(z_dst, y)
        buf[rows, :] = (
            buf[rows, :].astype(jnp.float32) + landed.astype(jnp.float32)
        ).astype(jnp.bfloat16)

    def add_two(buf, z_dst, first, second):
        rows = block(z_dst, y)
        buf[rows, :] = (
            buf[rows, :].astype(jnp.float32)
            + first.astype(jnp.float32)
            + second.astype(jnp.float32)
        ).astype(jnp.bfloat16)

    def reduce_step(buf, which, k):
        z_dst = order[k]
        reduce_pair(buf, which, z_dst).wait_recv()

        @pl.when(z < z_dst)
        def _():
            @pl.when(z > 0)
            def _():
                reduce_line(buf, which, 0, z_dst).wait_recv()
                add_two(buf, z_dst, from_pair[which, z_dst], from_left[which, z_dst])

            @pl.when(z == 0)
            def _():
                add_in(buf, z_dst, from_pair[which, z_dst])

            reduce_line(buf, which, 0, z_dst).start()

        @pl.when(z > z_dst)
        def _():
            @pl.when(z < outer - 1)
            def _():
                reduce_line(buf, which, 1, z_dst).wait_recv()
                add_two(buf, z_dst, from_pair[which, z_dst], from_right[which, z_dst])

            @pl.when(z == outer - 1)
            def _():
                add_in(buf, z_dst, from_pair[which, z_dst])

            reduce_line(buf, which, 1, z_dst).start()

    def reduce_finish(buf, which, total):
        total[...] = buf[block(z, y), :].astype(jnp.float32) + from_pair[which, z].astype(
            jnp.float32
        )

        @pl.when(z > 0)
        def _():
            reduce_line(buf, which, 0, z).wait_recv()
            total[...] += from_left[which, z].astype(jnp.float32)

        @pl.when(z < outer - 1)
        def _():
            reduce_line(buf, which, 1, z).wait_recv()
            total[...] += from_right[which, z].astype(jnp.float32)

    def reduce_drain(buf, which):
        for z_dst in range(outer):
            reduce_pair(buf, which, z_dst).wait_send()

            @pl.when(z < z_dst)
            def _():
                reduce_line(buf, which, 0, z_dst).wait_send()

            @pl.when(z > z_dst)
            def _():
                reduce_line(buf, which, 1, z_dst).wait_send()

    def columns(index):
        return pl.ds(pl.multiple_of(index * share_cols, share_cols), share_cols)

    def frag_copy(j):
        target = lax.rem(rep + j, replicas)
        return remote(
            fl_ref.at[:, :, columns(target)],
            pieces.at[j],
            frag_send.at[j],
            frag_recv.at[j],
            (target, me),
        )

    def new_copy(j):
        return remote(
            fresh,
            nl_ref.at[:, :, columns(rep)],
            new_send.at[j],
            new_recv.at[j],
            (lax.rem(rep + j, replicas), me),
        )

    def new_arrival(j):
        return remote(
            fresh,
            nl_ref.at[:, :, columns(lax.rem(rep + replicas - j, replicas))],
            new_send.at[j],
            new_recv.at[j],
            (lax.rem(rep + j, replicas), me),
        )

    def sqe_copy(j):
        return remote(
            sq_part.at[0],
            sq_exp.at[j],
            sqe_send.at[j],
            sqe_recv.at[j],
            (rep, lax.rem(me + j, groups)),
        )

    def sqr_copy(j):
        return remote(
            sq_part.at[1],
            sq_rep.at[j],
            sqr_send.at[j],
            sqr_recv.at[j],
            (lax.rem(rep + j, replicas), me),
        )

    mine = block(z, y)
    xs[mine, :] = x_ref[...]
    gather_step(xs, 0, 0)
    frag_order = [replicas // 2] + [j for j in range(1, replicas) if j != replicas // 2]
    for j in frag_order:
        frag_copy(j).start()
    own_piece = pltpu.make_async_copy(fl_ref.at[:, :, columns(rep)], pieces.at[0], frag_own_sem)
    own_piece.start()
    ys[mine, :] = dy_ref[...]
    for hop in range(1, outer - 1):
        gather_step(xs, 0, hop)
    gather_step(ys, 1, 0)
    gather_step(xs, 0, outer - 1)
    loads[0].wait()
    loads[1].wait()
    gather_finish(xs, 0)

    tiles = width // COLS

    def tile(index):
        return pl.ds(pl.multiple_of(index * COLS, COLS), COLS)

    pre[...] = jnp.zeros_like(pre)

    @pl.loop(0, tiles)
    def _(t):
        pre[...] += jnp.dot(xs[:, tile(t)], wgu[tile(t), :], preferred_element_type=jnp.float32)

    gate_pre = pre[:, :hidden]
    silu_val, _ = silu_parts(gate_pre)
    act = (silu_val * pre[:, hidden:]).astype(jnp.bfloat16)
    hid[...] = act
    act_t[...] = act.astype(jnp.float32).T.astype(jnp.bfloat16)
    loads[2].wait()

    @pl.loop(0, tiles)
    def _(t):
        part[:, tile(t)] = jnp.dot(
            hid[...], wd[:, tile(t)], preferred_element_type=jnp.float32
        ).astype(jnp.bfloat16)

    reduce_start(part, 0)
    gather_step(ys, 1, 1)

    loads[3].wait()
    own_piece.wait()
    for j in range(1, replicas):
        frag_copy(j).wait_recv()
    chunk = 32 if frag_rows % 32 == 0 else 16
    lanes = []
    for f in range(frags):

        def accumulate(i, total, f=f):
            rows = pl.ds(pl.multiple_of(i * chunk, chunk), chunk)
            summed = pieces[0, f, rows, :].astype(jnp.float32)
            for j in range(1, replicas):
                summed += pieces[j, f, rows, :].astype(jnp.float32)
            value = fg[f, rows, :] - summed * (1.0 / replicas)
            pseudo[f, rows, :] = value
            return total + jnp.sum(value * value, axis=0, keepdims=True)

        total = lax.fori_loop(
            0, frag_rows // chunk, accumulate, jnp.zeros((1, share_cols), jnp.float32)
        )
        lanes.append(jnp.sum(total, axis=1, keepdims=True))
    row_ids = lax.broadcasted_iota(jnp.int32, (8, 128), 0)
    tile_sum = jnp.zeros((8, 128), jnp.float32)
    for f in range(frags):
        tile_sum = jnp.where(row_ids == f, lanes[f], tile_sum)
    sq_part[0] = tile_sum
    for j in range(1, groups):
        sqe_copy(j).start()

    reduce_step(part, 0, 0)
    gather_step(ys, 1, 2)
    reduce_step(part, 0, 1)
    for hop in range(3, outer):
        gather_step(ys, 1, hop)

    for j in range(1, groups):
        sqe_copy(j).wait_recv()
    over_experts = sq_part[0]
    for j in range(1, groups):
        over_experts += sq_exp[j]
    sq_part[1] = over_experts
    for j in range(1, replicas):
        sqr_copy(j).start()
    for k in range(2, outer):
        reduce_step(part, 0, k)
    gather_finish(ys, 1)

    pre_dact = ggu.at[0]
    pre_dact[...] = jnp.zeros_like(pre_dact)

    @pl.loop(0, tiles)
    def _(t):
        pre_dact[...] += lax.dot_general(
            ys[:, tile(t)], wd[:, tile(t)], NT, preferred_element_type=jnp.float32
        )

    grad_hidden = pre_dact[...]
    silu_val, silu_slope = silu_parts(pre[:, :hidden])
    dpre[:, :hidden] = (grad_hidden * pre[:, hidden:] * silu_slope).astype(jnp.bfloat16)
    dpre[:, hidden:] = (grad_hidden * silu_val).astype(jnp.bfloat16)

    @pl.loop(0, tiles)
    def _(t):
        part_dx[:, tile(t)] = lax.dot_general(
            dpre[...], wgu[tile(t), :], NT, preferred_element_type=jnp.float32
        ).astype(jnp.bfloat16)

    reduce_start(part_dx, 1)

    loads[4].wait()
    for j in range(1, replicas):
        sqr_copy(j).wait_recv()
    squares = sq_part[1]
    for j in range(1, replicas):
        squares += sq_rep[j]
    limit = CLIP_RMS * (HID * D) ** 0.5
    factors = jnp.minimum(jnp.float32(1.0), limit / (jnp.sqrt(squares) + 1e-06))
    for f in range(frags):
        factor = factors[f : f + 1, :1]

        def update(i, carry, f=f, factor=factor):
            rows = pl.ds(pl.multiple_of(i * chunk, chunk), chunk)
            clipped = pseudo[f, rows, :] * factor
            moment = OUTER_MOMENTUM * fm[f, rows, :] + clipped
            anchor = fg[f, rows, :] - OUTER_RATE * (OUTER_MOMENTUM * moment + clipped)
            fm[f, rows, :] = moment
            fg[f, rows, :] = anchor
            fresh[f, rows, :] = anchor.astype(jnp.bfloat16)
            return carry

        lax.fori_loop(0, frag_rows // chunk, update, 0)
    for j in frag_order:
        new_copy(j).start()
    own_new = pltpu.make_async_copy(fresh, nl_ref.at[:, :, columns(rep)], new_own_sem)
    own_new.start()
    stores = [
        pltpu.make_async_copy(fg, ng_ref, store_sem.at[0]),
        pltpu.make_async_copy(fm, nm_ref, store_sem.at[1]),
    ]
    for store in stores:
        store.start()

    reduce_finish(part, 0, rows_ref)
    rows_ref[...] = rows_ref[...] * share_ref[...]
    reduce_step(part_dx, 1, 0)
    reduce_step(part_dx, 1, 1)

    @pl.loop(0, tiles)
    def _(t):
        both = lax.dot_general(
            xs[:, tile(t)], dpre[...], TN, preferred_element_type=jnp.float32
        ).astype(jnp.bfloat16)
        gdn[0, tile(t), :] = both[:, :hidden]
        gdn[1, tile(t), :] = both[:, hidden:]

    more = [
        pltpu.make_async_copy(gdn.at[0], gg_ref, store_sem.at[2]),
        pltpu.make_async_copy(gdn.at[1], gu_ref, store_sem.at[3]),
    ]
    for store in more:
        store.start()
    for k in range(2, outer):
        reduce_step(part_dx, 1, k)
    gd_out = wd

    @pl.loop(0, tiles)
    def _(t):
        gd_out[:, tile(t)] = jnp.dot(
            act_t[...], ys[:, tile(t)], preferred_element_type=jnp.float32
        ).astype(jnp.bfloat16)

    last = pltpu.make_async_copy(gd_out, gd_ref, store_sem.at[4])
    last.start()

    reduce_finish(part_dx, 1, dx_ref)

    for buf, which in ((xs, 0), (ys, 1)):
        gather_drain(buf, which)
    for buf, which in ((part, 0), (part_dx, 1)):
        reduce_drain(buf, which)
    for j in range(1, groups):
        sqe_copy(j).wait_send()
    for j in range(1, replicas):
        frag_copy(j).wait_send()
        sqr_copy(j).wait_send()
        new_copy(j).wait_send()
        new_arrival(j).wait_recv()
    own_new.wait()
    for store in stores + more + [last]:
        store.wait()


def pair_body(
    tokens, routes, cweights, w_gate, w_up, w_down, grad_out, frag_local, frag_global, frag_moment
):
    groups = lax.axis_size("expert")
    replicas = lax.axis_size("replica")
    inputs, grads_in = tokens[0], grad_out[0]
    width = inputs.shape[1]
    hidden = w_down.shape[1]
    frags, frag_rows, cols = frag_global.shape
    matched = routes[0] == 0
    routed = jnp.any(matched, axis=1)
    share = jnp.sum(jnp.where(matched, cweights[0], jnp.float32(0.0)), axis=1)
    ahead = jnp.arange(routed.shape[0], dtype=jnp.int32)
    earlier = (ahead[None, :] <= ahead[:, None]) & routed[None, :]
    places = jnp.sum(earlier.astype(jnp.int32), axis=1) - 1
    slot_ids = jnp.arange(CAP, dtype=jnp.int32)
    layout = routed[None, :] & (places[None, :] == slot_ids[:, None])
    layout_b = layout.astype(jnp.bfloat16)
    slot_share = jnp.sum(jnp.where(layout, share[None, :], 0.0), axis=1, keepdims=True)
    picked = jnp.dot(layout_b, inputs, preferred_element_type=jnp.float32).astype(jnp.bfloat16)
    dy = jnp.dot(layout_b, grads_in, preferred_element_type=jnp.float32)
    dy = (dy * slot_share).astype(jnp.bfloat16)
    bf, f32 = jnp.bfloat16, jnp.float32
    outer = groups // INNER
    total = groups * CAP
    dma = pltpu.SemaphoreType.DMA
    vmem, hbm = pl.BlockSpec(memory_space=pltpu.VMEM), pl.BlockSpec(memory_space=pl.ANY)
    shape = jax.ShapeDtypeStruct
    rows, dx, gg, gu, gd, ng, nm, nl = pl.pallas_call(
        functools.partial(step_kernel, groups, replicas),
        out_shape=(
            shape((CAP, width), f32),
            shape((CAP, width), f32),
            shape((width, hidden), bf),
            shape((width, hidden), bf),
            shape((hidden, width), bf),
            shape(frag_global.shape, f32),
            shape(frag_global.shape, f32),
            shape(frag_local.shape[1:], bf),
        ),
        in_specs=[vmem] * 3 + [hbm] * 6,
        out_specs=(vmem,) * 2 + (hbm,) * 6,
        scratch_shapes=[
            pltpu.VMEM((total, width), bf),
            pltpu.VMEM((total, width), bf),
            pltpu.VMEM((total, width), bf),
            pltpu.VMEM((total, width), bf),
            pltpu.VMEM((2, outer, CAP, width), bf),
            pltpu.VMEM((2, outer, CAP, width), bf),
            pltpu.VMEM((2, outer, CAP, width), bf),
            pltpu.VMEM((width, 2 * hidden), bf),
            pltpu.VMEM((hidden, width), bf),
            pltpu.VMEM((total, 2 * hidden), f32),
            pltpu.VMEM((total, hidden), bf),
            pltpu.VMEM((hidden, total), bf),
            pltpu.VMEM((total, 2 * hidden), bf),
            pltpu.VMEM((1, total, hidden), f32),
            pltpu.VMEM((2, width, hidden), bf),
            pltpu.VMEM((replicas, frags, frag_rows, cols), bf),
            pltpu.VMEM(frag_global.shape, f32),
            pltpu.VMEM(frag_global.shape, f32),
            pltpu.VMEM(frag_global.shape, f32),
            pltpu.VMEM(frag_global.shape, bf),
            pltpu.VMEM((2, 8, 128), f32),
            pltpu.VMEM((groups, 8, 128), f32),
            pltpu.VMEM((replicas, 8, 128), f32),
            dma((5,)),
            dma((5,)),
            dma((2, 2, outer)),
            dma((2, 2, outer)),
            dma((2, outer)),
            dma((2, outer)),
            dma((2, 2, outer)),
            dma((2, 2, outer)),
            dma((2, outer)),
            dma((2, outer)),
            dma((replicas,)),
            dma((replicas,)),
            dma,
            dma((groups,)),
            dma((groups,)),
            dma((replicas,)),
            dma((replicas,)),
            dma((replicas,)),
            dma((replicas,)),
            dma,
        ],
        compiler_params=pltpu.CompilerParams(
            collective_id=0, has_side_effects=True, vmem_limit_bytes=56 * 2**20
        ),
    )(
        picked,
        dy,
        slot_share,
        w_gate[0],
        w_up[0],
        w_down[0],
        frag_local[0],
        frag_global,
        frag_moment,
    )
    back = layout_b.T
    layer_out = jnp.dot(back, rows.astype(bf), preferred_element_type=f32).astype(bf)
    grad_tokens = jnp.dot(back, dx.astype(bf), preferred_element_type=f32).astype(bf)
    return (layer_out[None], grad_tokens[None], gg[None], gu[None], gd[None], ng, nm, nl[None])


def body(*operands):
    if lax.axis_size("expert") == SPLIT:
        return pair_body(*operands)
    return general_body(*operands)


def solution(mesh):
    return jax.shard_map(
        body,
        mesh=mesh,
        in_specs=(
            P("replica", "expert", None),
            P("replica", "expert", None),
            P("replica", "expert", None),
            P("replica", None, "expert"),
            P("replica", None, "expert"),
            P("replica", "expert", None),
            P("replica", "expert", None),
            P("replica", None, "expert", None),
            P(None, "expert", "replica"),
            P(None, "expert", "replica"),
        ),
        out_specs=(
            P("replica", "expert", None),
            P("replica", "expert", None),
            P("replica", None, "expert"),
            P("replica", None, "expert"),
            P("replica", "expert", None),
            P(None, "expert", "replica"),
            P(None, "expert", "replica"),
            P("replica", None, "expert", None),
        ),
        check_vma=False,
    )
```

```python
import functools

import jax
import jax.numpy as jnp
from jax import lax
from jax.experimental import pallas as pl
from jax.experimental.pallas import tpu as pltpu
from jax.sharding import PartitionSpec as P

D = 4096
HID = 1024
SPLIT = 8
CAP = 32


OUTER_MOMENTUM = 0.9
OUTER_RATE = 0.7
CLIP_RMS = 0.5


def silu_parts(gate_pre):
    sigmoid_val = jax.nn.sigmoid(gate_pre)
    return (gate_pre * sigmoid_val, sigmoid_val * (1.0 + gate_pre * (1.0 - sigmoid_val)))


def outer_update(pseudo, squares, moment, anchor):
    clip_limit = CLIP_RMS * (HID * D) ** 0.5
    factor = jnp.minimum(jnp.float32(1.0), clip_limit / (jnp.sqrt(squares) + 1e-06))
    clipped = pseudo * factor[:, None, None]
    moment_next = OUTER_MOMENTUM * moment + clipped
    anchor_next = anchor - OUTER_RATE * (OUTER_MOMENTUM * moment_next + clipped)
    return (moment_next, anchor_next)


def general_body(
    tokens, routes, cweights, w_gate, w_up, w_down, grad_out, frag_local, frag_global, frag_moment
):
    groups = lax.axis_size("expert")
    window = groups // SPLIT
    precise = lax.Precision.HIGHEST
    inputs = tokens[0]
    grads_in = grad_out[0]
    route_ids = routes[0]
    weights = cweights[0]
    wg_part = w_gate[0]
    wu_part = w_up[0]
    wd_part = w_down[0]
    model_width = inputs.shape[1]
    experts = jnp.arange(window, dtype=jnp.int32)
    matched = route_ids[:, :, None] == experts[None, None, :]
    routed = jnp.any(matched, axis=1).astype(jnp.int32)
    shares = jnp.sum(jnp.where(matched, weights[:, :, None], jnp.float32(0.0)), axis=1)
    places = jnp.cumsum(routed, axis=0) - 1
    slot_ids = jnp.arange(CAP, dtype=jnp.int32)
    layout = (routed.T[:, None, :] == 1) & (places.T[:, None, :] == slot_ids[None, :, None])
    layout_f = layout.astype(jnp.float32)
    layout_b = layout.astype(jnp.bfloat16)
    combine = layout_f * shares.T[:, None, :]
    slot_share = jnp.sum(combine, axis=2)
    picked = jnp.einsum("ect,td->ecd", layout_b, inputs, preferred_element_type=jnp.float32).astype(
        jnp.bfloat16
    )
    outbound = jnp.broadcast_to(picked[:, None], (window, SPLIT, CAP, model_width)).reshape(
        groups, CAP, model_width
    )
    received = lax.all_to_all(outbound, "expert", split_axis=0, concat_axis=0, tiled=True)
    n_source, n_rows, width_in = received.shape
    flat = received.reshape(n_source * n_rows, width_in)
    gate_pre = jnp.dot(flat, wg_part, preferred_element_type=jnp.float32)
    up_pre = jnp.dot(flat, wu_part, preferred_element_type=jnp.float32)
    silu_val, silu_slope = silu_parts(gate_pre)
    hidden_act = (silu_val * up_pre).astype(jnp.bfloat16)
    partial_value = jnp.dot(hidden_act, wd_part, preferred_element_type=jnp.float32)
    partial_out, hidden_act, gate_pre, up_pre, rows_in = (
        partial_value.reshape(n_source, n_rows, width_in),
        hidden_act.reshape(n_source, n_rows, -1),
        gate_pre.reshape(n_source, n_rows, -1),
        up_pre.reshape(n_source, n_rows, -1),
        received,
    )
    returned = lax.all_to_all(partial_out, "expert", split_axis=0, concat_axis=0, tiled=True)
    expert_out = jnp.sum(returned.reshape(window, SPLIT, CAP, model_width), axis=1)
    layer_out = jnp.einsum(
        "ect,ecd->td", combine, expert_out, precision=precise, preferred_element_type=jnp.float32
    ).astype(jnp.bfloat16)
    dy_picked = jnp.einsum("ect,td->ecd", layout_b, grads_in, preferred_element_type=jnp.float32)
    dy_scaled = (dy_picked * slot_share[:, :, None]).astype(jnp.bfloat16)
    outbound_dy = jnp.broadcast_to(dy_scaled[:, None], (window, SPLIT, CAP, model_width)).reshape(
        groups, CAP, model_width
    )
    rows_dy = lax.all_to_all(outbound_dy, "expert", split_axis=0, concat_axis=0, tiled=True)
    grad_rows = rows_dy.reshape(-1, model_width)
    tok_rows = rows_in.reshape(-1, model_width)
    act_rows = hidden_act.reshape(grad_rows.shape[0], -1)
    gate_rows = gate_pre.reshape(grad_rows.shape[0], -1)
    up_rows = up_pre.reshape(grad_rows.shape[0], -1)
    grad_hidden = jnp.einsum("rd,hd->rh", grad_rows, wd_part, preferred_element_type=jnp.float32)
    silu_val, silu_slope = silu_parts(gate_rows)
    grad_gate_pre = (grad_hidden * up_rows * silu_slope).astype(jnp.bfloat16)
    grad_up_pre = (grad_hidden * silu_val).astype(jnp.bfloat16)
    grad_gate = jnp.einsum(
        "rd,rh->dh", tok_rows, grad_gate_pre, preferred_element_type=jnp.float32
    ).astype(jnp.bfloat16)[None]
    grad_up = jnp.einsum(
        "rd,rh->dh", tok_rows, grad_up_pre, preferred_element_type=jnp.float32
    ).astype(jnp.bfloat16)[None]
    grad_down = jnp.einsum(
        "rh,rd->hd", act_rows, grad_rows, preferred_element_type=jnp.float32
    ).astype(jnp.bfloat16)[None]
    partial_dx = jnp.einsum(
        "rh,dh->rd", grad_gate_pre, wg_part, preferred_element_type=jnp.float32
    ) + jnp.einsum("rh,dh->rd", grad_up_pre, wu_part, preferred_element_type=jnp.float32)
    partial_dx = partial_dx.reshape(groups, CAP, model_width)
    returned_dx = lax.all_to_all(partial_dx, "expert", split_axis=0, concat_axis=0, tiled=True)
    expert_dx = jnp.sum(returned_dx.reshape(window, SPLIT, CAP, model_width), axis=1)
    grad_tokens = jnp.einsum(
        "ect,ecd->td", layout_f, expert_dx, precision=precise, preferred_element_type=jnp.float32
    ).astype(jnp.bfloat16)
    replicas = lax.axis_size("replica")
    local_terms = frag_local[0].astype(jnp.float32)
    summed = lax.psum_scatter(
        local_terms.astype(jnp.bfloat16), "replica", scatter_dimension=2, tiled=True
    ).astype(jnp.float32)
    pseudo = frag_global - summed / replicas
    squares = lax.psum(jnp.sum(pseudo * pseudo, axis=(1, 2)), ("replica", "expert"))
    new_moment, new_global = outer_update(pseudo, squares, frag_moment, frag_global)
    new_local = lax.all_gather(new_global.astype(jnp.bfloat16), "replica", axis=2, tiled=True)[None]
    return (
        layer_out[None],
        grad_tokens[None],
        grad_gate,
        grad_up,
        grad_down,
        new_global,
        new_moment,
        new_local,
    )


MESH = pl.DeviceIdType.MESH
INNER = 2
COLS = 512
SPLITS = ((3584, 2560), (2560, 3584))
NT = (((1,), (1,)), ((), ()))
TN = (((0,), (0,)), ((), ()))


def step_kernel(
    groups,
    replicas,
    splits,
    x_ref,
    routes_ref,
    weights_ref,
    dy_ref,
    wg_ref,
    wu_ref,
    wd_ref,
    fl_ref,
    fg_ref,
    fm_ref,
    lo_ref,
    gt_ref,
    gg_ref,
    gu_ref,
    gd_ref,
    ng_ref,
    nm_ref,
    nl_ref,
    xs,
    ys,
    part,
    part_dx,
    from_pair,
    from_left,
    from_right,
    wgu,
    wd,
    pre,
    hid,
    act_t,
    dpre,
    ggu,
    gdn,
    pieces,
    fg,
    fm,
    pseudo,
    fresh,
    sq_part,
    sq_exp,
    sq_rep,
    total,
    placed,
    grads,
    load_sem,
    store_sem,
    gather_send,
    gather_recv,
    gpair_send,
    gpair_recv,
    red_send,
    red_recv,
    rpair_send,
    rpair_recv,
    frag_send,
    frag_recv,
    frag_own_sem,
    sqe_send,
    sqe_recv,
    sqr_send,
    sqr_recv,
    new_send,
    new_recv,
    new_own_sem,
):
    rep = lax.axis_index("replica")
    me = lax.axis_index("expert")
    outer = groups // INNER
    z = me // INNER
    y = me % INNER
    pair = z * INNER + (1 - y)
    width = x_ref.shape[1]
    hidden = wd_ref.shape[0]
    share_cols = fg_ref.shape[2]
    frags = fg_ref.shape[0]
    frag_rows = fg_ref.shape[1]

    loads = [
        pltpu.make_async_copy(wg_ref, wgu.at[:, pl.ds(0, hidden)], load_sem.at[0]),
        pltpu.make_async_copy(wu_ref, wgu.at[:, pl.ds(hidden, hidden)], load_sem.at[1]),
        pltpu.make_async_copy(wd_ref, wd, load_sem.at[2]),
        pltpu.make_async_copy(fg_ref, fg, load_sem.at[3]),
        pltpu.make_async_copy(fm_ref, fm, load_sem.at[4]),
        pltpu.make_async_copy(dy_ref, grads, load_sem.at[5]),
    ]
    for load in loads:
        load.start()

    barrier = pltpu.get_barrier_semaphore()
    for j in range(1, groups):
        pl.semaphore_signal(
            barrier, inc=1, device_id=(rep, lax.rem(me + j, groups)), device_id_type=MESH
        )
    for j in range(1, replicas):
        pl.semaphore_signal(
            barrier, inc=1, device_id=(lax.rem(rep + j, replicas), me), device_id_type=MESH
        )
    def block(z_of, y_of):
        return pl.ds(pl.multiple_of((z_of * INNER + y_of) * CAP, CAP), CAP)

    def remote(src, dst, send, recv, target):
        return pltpu.make_async_remote_copy(
            src_ref=src,
            dst_ref=dst,
            send_sem=send,
            recv_sem=recv,
            device_id=target,
            device_id_type=MESH,
        )

    def right():
        return (rep, jnp.minimum(z + 1, outer - 1) * INNER + y)

    def left():
        return (rep, jnp.maximum(z - 1, 0) * INNER + y)

    def near(which, gather):
        return pl.ds(0, splits[gather][which])

    def far(which, gather):
        return pl.ds(splits[gather][which], width - splits[gather][which])

    def toward(way):
        return right() if way == 0 else left()

    def other(stream):
        return y if stream == 0 else 1 - y

    def gather_copy(buf, which, way, hop, z_src, stream):
        cols = near(which, 0) if stream == 2 else far(which, 0)
        rows = buf.at[block(z_src, y if stream == 2 else other(stream)), cols]
        return remote(
            rows,
            rows,
            gather_send.at[which, way, stream, hop],
            gather_recv.at[which, way, stream, hop],
            toward(way),
        )

    def gather_pair(buf, which, z_src, y_src):
        rows = buf.at[block(z_src, y_src), near(which, 0)]
        return remote(
            rows, rows, gpair_send.at[which, z_src], gpair_recv.at[which, z_src], (rep, pair)
        )

    def gather_swap(buf, which, y_src):
        rows = buf.at[block(z, y_src), far(which, 0)]
        return remote(
            rows, rows, gpair_send.at[which, outer], gpair_recv.at[which, outer], (rep, pair)
        )

    def gather_both_ways(buf, which, stream):
        @pl.when(z < outer - 1)
        def _():
            gather_copy(buf, which, 0, 0, z, stream).start()

        @pl.when(z > 0)
        def _():
            gather_copy(buf, which, 1, 0, z, stream).start()

    def gather_start(buf, which):
        gather_swap(buf, which, y).start()
        gather_both_ways(buf, which, 2)
        gather_pair(buf, which, z, y).start()
        gather_both_ways(buf, which, 0)

    def gather_turn(buf, which):
        gather_swap(buf, which, 1 - y).wait_recv()
        gather_both_ways(buf, which, 1)

    def gather_step(buf, which, hop):
        for stream in (2, 0, 1):

            @pl.when(z >= hop)
            def _(stream=stream):
                gather_copy(buf, which, 0, hop - 1, z - hop, stream).wait_recv()
                if hop < outer - 1:

                    @pl.when(z < outer - 1)
                    def _():
                        gather_copy(buf, which, 0, hop, z - hop, stream).start()

                if stream == 2:
                    gather_pair(buf, which, z - hop, y).start()

            @pl.when(z + hop < outer)
            def _(stream=stream):
                gather_copy(buf, which, 1, hop - 1, z + hop, stream).wait_recv()
                if hop < outer - 1:

                    @pl.when(z > 0)
                    def _():
                        gather_copy(buf, which, 1, hop, z + hop, stream).start()

                if stream == 2:
                    gather_pair(buf, which, z + hop, y).start()

    def gather_finish(buf, which):
        for z_src in range(outer):
            gather_pair(buf, which, z_src, 1 - y).wait_recv()

    def gather_drain(buf, which):
        for stream in range(3):
            for hop in range(outer - 1):

                @pl.when((z < outer - 1) & (z >= hop))
                def _(stream=stream, hop=hop):
                    gather_copy(buf, which, 0, hop, z - hop, stream).wait_send()

                @pl.when((z > 0) & (z + hop < outer))
                def _(stream=stream, hop=hop):
                    gather_copy(buf, which, 1, hop, z + hop, stream).wait_send()

        for z_src in range(outer):
            gather_pair(buf, which, z_src, y).wait_send()
        gather_swap(buf, which, y).wait_send()

    order = []
    for k in range(outer // 2):
        order += [outer - 1 - k, k]
    if outer % 2:
        order.append(outer // 2)

    def reduce_pair(buf, which, z_dst):
        return remote(
            buf.at[block(z_dst, 1 - y), near(which, 1)],
            from_pair.at[which, z_dst, :, near(which, 1)],
            rpair_send.at[which, z_dst],
            rpair_recv.at[which, z_dst],
            (rep, pair),
        )

    def reduce_swap(buf, which):
        return remote(
            buf.at[block(z, 1 - y), far(which, 1)],
            from_pair.at[which, z, :, far(which, 1)],
            rpair_send.at[which, outer],
            rpair_recv.at[which, outer],
            (rep, pair),
        )

    def landing(which, way, z_dst, stream):
        held = from_left if way == 0 else from_right
        cols = near(which, 1) if stream == 2 else far(which, 1)
        return held.at[which, 1 if stream == 1 else 0, z_dst, :, cols]

    def home(buf, which, z_dst, stream):
        cols = near(which, 1) if stream == 2 else far(which, 1)
        return buf.at[block(z_dst, y if stream == 2 else other(stream)), cols]

    def reduce_line(buf, which, way, z_dst, stream):
        return remote(
            home(buf, which, z_dst, stream),
            landing(which, way, z_dst, stream),
            red_send.at[which, way, stream, z_dst],
            red_recv.at[which, way, stream, z_dst],
            toward(way),
        )

    def reduce_start(buf, which):
        for z_dst in order:
            reduce_pair(buf, which, z_dst).start()

    def add_to(target, *terms):
        value = target[...].astype(jnp.float32)
        for term in terms:
            value = value + term[...].astype(jnp.float32)
        target[...] = value.astype(jnp.bfloat16)

    def reduce_step(buf, which, k, streams=(1, 0, 2)):
        z_dst = order[k]
        for stream in streams:
            pair_term = ()
            if stream == 2:
                reduce_pair(buf, which, z_dst).wait_recv()
                pair_term = (from_pair.at[which, z_dst, :, near(which, 1)],)
            target = home(buf, which, z_dst, stream)
            for way, ahead, behind in (
                (0, z < z_dst, z > 0),
                (1, z > z_dst, z < outer - 1),
            ):

                @pl.when(ahead & behind)
                def _(way=way, stream=stream, target=target, pair_term=pair_term):
                    reduce_line(buf, which, way, z_dst, stream).wait_recv()
                    add_to(target, landing(which, way, z_dst, stream), *pair_term)

                if stream == 2:

                    @pl.when(ahead & jnp.logical_not(behind))
                    def _(target=target, pair_term=pair_term):
                        add_to(target, *pair_term)

                @pl.when(ahead)
                def _(way=way, stream=stream):
                    reduce_line(buf, which, way, z_dst, stream).start()

    def reduce_turn(buf, which):
        target = home(buf, which, z, 1)

        @pl.when(z > 0)
        def _():
            reduce_line(buf, which, 0, z, 1).wait_recv()
            add_to(target, landing(which, 0, z, 1))

        @pl.when(z < outer - 1)
        def _():
            reduce_line(buf, which, 1, z, 1).wait_recv()
            add_to(target, landing(which, 1, z, 1))

        reduce_swap(buf, which).start()

    def reduce_finish(buf, which):
        for stream in (2, 0):
            cols = near(which, 1) if stream == 2 else far(which, 1)
            total[:, cols] = home(buf, which, z, stream)[...].astype(jnp.float32)

            @pl.when(z > 0)
            def _(stream=stream, cols=cols):
                reduce_line(buf, which, 0, z, stream).wait_recv()
                total[:, cols] += landing(which, 0, z, stream)[...].astype(jnp.float32)

            @pl.when(z < outer - 1)
            def _(stream=stream, cols=cols):
                reduce_line(buf, which, 1, z, stream).wait_recv()
                total[:, cols] += landing(which, 1, z, stream)[...].astype(jnp.float32)

        reduce_swap(buf, which).wait_recv()
        total[...] += from_pair[which, z].astype(jnp.float32)

    def reduce_drain(buf, which):
        for z_dst in range(outer):
            reduce_pair(buf, which, z_dst).wait_send()
            for stream in range(3):

                @pl.when(z < z_dst)
                def _(stream=stream, z_dst=z_dst):
                    reduce_line(buf, which, 0, z_dst, stream).wait_send()

                @pl.when(z > z_dst)
                def _(stream=stream, z_dst=z_dst):
                    reduce_line(buf, which, 1, z_dst, stream).wait_send()

        reduce_swap(buf, which).wait_send()

    def columns(index):
        return pl.ds(pl.multiple_of(index * share_cols, share_cols), share_cols)

    def frag_copy(j):
        target = lax.rem(rep + j, replicas)
        return remote(
            fl_ref.at[:, :, columns(target)],
            pieces.at[j],
            frag_send.at[j],
            frag_recv.at[j],
            (target, me),
        )

    def new_copy(j):
        return remote(
            fresh,
            nl_ref.at[:, :, columns(rep)],
            new_send.at[j],
            new_recv.at[j],
            (lax.rem(rep + j, replicas), me),
        )

    def new_arrival(j):
        return remote(
            fresh,
            nl_ref.at[:, :, columns(lax.rem(rep + replicas - j, replicas))],
            new_send.at[j],
            new_recv.at[j],
            (lax.rem(rep + j, replicas), me),
        )

    def sqe_copy(j):
        return remote(
            sq_part.at[0],
            sq_exp.at[j],
            sqe_send.at[j],
            sqe_recv.at[j],
            (rep, lax.rem(me + j, groups)),
        )

    def sqr_copy(j):
        return remote(
            sq_part.at[1],
            sq_rep.at[j],
            sqr_send.at[j],
            sqr_recv.at[j],
            (lax.rem(rep + j, replicas), me),
        )

    tiles = width // COLS

    def tile(index):
        return pl.ds(pl.multiple_of(index * COLS, COLS), COLS)

    count = x_ref.shape[0]
    matched = routes_ref[...] == 0
    flags = jnp.sum(matched.astype(jnp.float32), axis=1, keepdims=True)
    shares = jnp.sum(
        jnp.where(matched, weights_ref[...], jnp.float32(0.0)), axis=1, keepdims=True
    )
    flag_row = jnp.broadcast_to(flags, (count, count)).T
    share_row = jnp.broadcast_to(shares, (count, count)).T[:CAP]
    before = lax.broadcasted_iota(jnp.int32, (count, count), 0)
    after = lax.broadcasted_iota(jnp.int32, (count, count), 1)
    upper = (before < after).astype(jnp.bfloat16)
    flag_row = flag_row[:CAP]
    places = jnp.dot(flag_row.astype(jnp.bfloat16), upper, preferred_element_type=jnp.float32)
    slots = lax.broadcasted_iota(jnp.int32, (CAP, count), 0).astype(jnp.float32)
    chosen = (flag_row > 0.5) & (places == slots)
    layout = chosen.astype(jnp.float32).astype(jnp.bfloat16)
    slot_share = jnp.sum(jnp.where(chosen, share_row, 0.0), axis=1, keepdims=True)

    mine = block(z, y)

    @pl.loop(0, tiles)
    def _(t):
        xs[mine, tile(t)] = jnp.dot(
            layout, x_ref[:, tile(t)], preferred_element_type=jnp.float32
        ).astype(jnp.bfloat16)

    pl.semaphore_wait(barrier, groups - 1 + replicas - 1)
    gather_start(xs, 0)
    frag_order = [replicas // 2] + [j for j in range(1, replicas) if j != replicas // 2]
    for j in frag_order:
        frag_copy(j).start()
    own_piece = pltpu.make_async_copy(fl_ref.at[:, :, columns(rep)], pieces.at[0], frag_own_sem)
    own_piece.start()
    loads[5].wait()

    @pl.loop(0, tiles)
    def _(t):
        picked = jnp.dot(layout, grads[:, tile(t)], preferred_element_type=jnp.float32)
        ys[mine, tile(t)] = (picked * slot_share).astype(jnp.bfloat16)

    gather_turn(xs, 0)
    for hop in range(1, outer - 1):
        gather_step(xs, 0, hop)
    gather_start(ys, 1)
    gather_step(xs, 0, outer - 1)
    loads[0].wait()
    loads[1].wait()
    gather_finish(xs, 0)
    gather_turn(ys, 1)

    pre[...] = jnp.zeros_like(pre)

    @pl.loop(0, tiles)
    def _(t):
        pre[...] += jnp.dot(xs[:, tile(t)], wgu[tile(t), :], preferred_element_type=jnp.float32)

    gate_pre = pre[:, :hidden]
    silu_val, _ = silu_parts(gate_pre)
    act = (silu_val * pre[:, hidden:]).astype(jnp.bfloat16)
    hid[...] = act
    act_t[...] = act.astype(jnp.float32).T.astype(jnp.bfloat16)
    loads[2].wait()

    gather_step(ys, 1, 1)
    cut = splits[1][0] // COLS

    def forward(t):
        part[:, tile(t)] = jnp.dot(
            hid[...], wd[:, tile(t)], preferred_element_type=jnp.float32
        ).astype(jnp.bfloat16)

    pl.loop(0, cut)(forward)
    reduce_start(part, 0)
    pl.loop(cut, tiles)(forward)
    reduce_step(part, 0, 0, (1, 0))
    gather_step(ys, 1, 2)
    reduce_step(part, 0, 0, (2,))
    reduce_step(part, 0, 1)
    for hop in range(3, outer):
        gather_step(ys, 1, hop)

    loads[3].wait()
    own_piece.wait()
    for j in range(1, replicas):
        frag_copy(j).wait_recv()
    chunk = 32 if frag_rows % 32 == 0 else 16
    lanes = []
    for f in range(frags):

        def accumulate(i, total, f=f):
            rows = pl.ds(pl.multiple_of(i * chunk, chunk), chunk)
            summed = pieces[0, f, rows, :].astype(jnp.float32)
            for j in range(1, replicas):
                summed += pieces[j, f, rows, :].astype(jnp.float32)
            value = fg[f, rows, :] - summed * (1.0 / replicas)
            pseudo[f, rows, :] = value
            return total + jnp.sum(value * value, axis=0, keepdims=True)

        squared = lax.fori_loop(
            0, frag_rows // chunk, accumulate, jnp.zeros((1, share_cols), jnp.float32)
        )
        lanes.append(jnp.sum(squared, axis=1, keepdims=True))
    row_ids = lax.broadcasted_iota(jnp.int32, (8, 128), 0)
    tile_sum = jnp.zeros((8, 128), jnp.float32)
    for f in range(frags):
        tile_sum = jnp.where(row_ids == f, lanes[f], tile_sum)
    sq_part[0] = tile_sum
    for j in range(1, groups):
        sqe_copy(j).start()

    for k in range(2, outer):
        reduce_step(part, 0, k)
    reduce_turn(part, 0)
    gather_finish(ys, 1)

    for j in range(1, groups):
        sqe_copy(j).wait_recv()
    over_experts = sq_part[0]
    for j in range(1, groups):
        over_experts += sq_exp[j]
    sq_part[1] = over_experts
    for j in range(1, replicas):
        sqr_copy(j).start()

    pre_dact = ggu.at[0]
    pre_dact[...] = jnp.zeros_like(pre_dact)

    @pl.loop(0, tiles)
    def _(t):
        pre_dact[...] += lax.dot_general(
            ys[:, tile(t)], wd[:, tile(t)], NT, preferred_element_type=jnp.float32
        )

    grad_hidden = pre_dact[...]
    silu_val, silu_slope = silu_parts(pre[:, :hidden])
    dpre[:, :hidden] = (grad_hidden * pre[:, hidden:] * silu_slope).astype(jnp.bfloat16)
    dpre[:, hidden:] = (grad_hidden * silu_val).astype(jnp.bfloat16)

    cut_dx = splits[1][1] // COLS

    def backward(t):
        part_dx[:, tile(t)] = lax.dot_general(
            dpre[...], wgu[tile(t), :], NT, preferred_element_type=jnp.float32
        ).astype(jnp.bfloat16)

    pl.loop(0, cut_dx)(backward)
    reduce_start(part_dx, 1)
    pl.loop(cut_dx, tiles)(backward)
    reduce_step(part_dx, 1, 0, (1, 0))

    loads[4].wait()
    for j in range(1, replicas):
        sqr_copy(j).wait_recv()
    squares = sq_part[1]
    for j in range(1, replicas):
        squares += sq_rep[j]
    limit = CLIP_RMS * (HID * D) ** 0.5
    factors = jnp.minimum(jnp.float32(1.0), limit / (jnp.sqrt(squares) + 1e-06))
    for f in range(frags):
        factor = factors[f : f + 1, :1]

        def update(i, carry, f=f, factor=factor):
            rows = pl.ds(pl.multiple_of(i * chunk, chunk), chunk)
            clipped = pseudo[f, rows, :] * factor
            moment = OUTER_MOMENTUM * fm[f, rows, :] + clipped
            anchor = fg[f, rows, :] - OUTER_RATE * (OUTER_MOMENTUM * moment + clipped)
            fm[f, rows, :] = moment
            fg[f, rows, :] = anchor
            fresh[f, rows, :] = anchor.astype(jnp.bfloat16)
            return carry

        lax.fori_loop(0, frag_rows // chunk, update, 0)
    for j in frag_order:
        new_copy(j).start()
    own_new = pltpu.make_async_copy(fresh, nl_ref.at[:, :, columns(rep)], new_own_sem)
    own_new.start()
    stores = [
        pltpu.make_async_copy(fg, ng_ref, store_sem.at[0]),
        pltpu.make_async_copy(fm, nm_ref, store_sem.at[1]),
    ]
    for store in stores:
        store.start()

    def place(which, ref):
        total_b = total[...].astype(jnp.bfloat16)
        for t in range(tiles):
            cols = pl.ds(t * COLS, COLS)
            placed[which, :, cols] = lax.dot_general(
                layout,
                total_b[:, t * COLS : (t + 1) * COLS],
                TN,
                preferred_element_type=jnp.float32,
            ).astype(jnp.bfloat16)
        copy = pltpu.make_async_copy(placed.at[which], ref, store_sem.at[5 + which])
        copy.start()
        return copy

    reduce_step(part_dx, 1, 0, (2,))
    reduce_step(part_dx, 1, 1)
    reduce_finish(part, 0)
    total[...] = total[...] * slot_share
    placed_out = place(0, lo_ref)

    @pl.loop(0, tiles)
    def _(t):
        both = lax.dot_general(
            xs[:, tile(t)], dpre[...], TN, preferred_element_type=jnp.float32
        ).astype(jnp.bfloat16)
        gdn[0, tile(t), :] = both[:, :hidden]
        gdn[1, tile(t), :] = both[:, hidden:]

    more = [
        pltpu.make_async_copy(gdn.at[0], gg_ref, store_sem.at[2]),
        pltpu.make_async_copy(gdn.at[1], gu_ref, store_sem.at[3]),
    ]
    for store in more:
        store.start()
    for k in range(2, outer):
        reduce_step(part_dx, 1, k)
    reduce_turn(part_dx, 1)
    gd_out = wd

    @pl.loop(0, tiles)
    def _(t):
        gd_out[:, tile(t)] = jnp.dot(
            act_t[...], ys[:, tile(t)], preferred_element_type=jnp.float32
        ).astype(jnp.bfloat16)

    last = pltpu.make_async_copy(gd_out, gd_ref, store_sem.at[4])
    last.start()

    reduce_finish(part_dx, 1)
    placed_dx = place(1, gt_ref)

    for buf, which in ((xs, 0), (ys, 1)):
        gather_drain(buf, which)
    for buf, which in ((part, 0), (part_dx, 1)):
        reduce_drain(buf, which)
    for j in range(1, groups):
        sqe_copy(j).wait_send()
    for j in range(1, replicas):
        frag_copy(j).wait_send()
        sqr_copy(j).wait_send()
        new_copy(j).wait_send()
        new_arrival(j).wait_recv()
    own_new.wait()
    for store in stores + more + [last, placed_out, placed_dx]:
        store.wait()


def pair_body(
    tokens, routes, cweights, w_gate, w_up, w_down, grad_out, frag_local, frag_global, frag_moment
):
    groups = lax.axis_size("expert")
    replicas = lax.axis_size("replica")
    inputs, grads_in = tokens[0], grad_out[0]
    width = inputs.shape[1]
    hidden = w_down.shape[1]
    frags, frag_rows, cols = frag_global.shape
    bf, f32 = jnp.bfloat16, jnp.float32
    outer = groups // INNER
    total = groups * CAP
    dma = pltpu.SemaphoreType.DMA
    vmem, hbm = pl.BlockSpec(memory_space=pltpu.VMEM), pl.BlockSpec(memory_space=pl.ANY)
    shape = jax.ShapeDtypeStruct
    lo, gt, gg, gu, gd, ng, nm, nl = pl.pallas_call(
        functools.partial(step_kernel, groups, replicas, SPLITS),
        out_shape=(
            shape(inputs.shape, bf),
            shape(inputs.shape, bf),
            shape((width, hidden), bf),
            shape((width, hidden), bf),
            shape((hidden, width), bf),
            shape(frag_global.shape, f32),
            shape(frag_global.shape, f32),
            shape(frag_local.shape[1:], bf),
        ),
        in_specs=[vmem] * 3 + [hbm] * 7,
        out_specs=(hbm,) * 8,
        scratch_shapes=[
            pltpu.VMEM((total, width), bf),
            pltpu.VMEM((total, width), bf),
            pltpu.VMEM((total, width), bf),
            pltpu.VMEM((total, width), bf),
            pltpu.VMEM((2, outer, CAP, width), bf),
            pltpu.VMEM((2, 2, outer, CAP, width), bf),
            pltpu.VMEM((2, 2, outer, CAP, width), bf),
            pltpu.VMEM((width, 2 * hidden), bf),
            pltpu.VMEM((hidden, width), bf),
            pltpu.VMEM((total, 2 * hidden), f32),
            pltpu.VMEM((total, hidden), bf),
            pltpu.VMEM((hidden, total), bf),
            pltpu.VMEM((total, 2 * hidden), bf),
            pltpu.VMEM((1, total, hidden), f32),
            pltpu.VMEM((2, width, hidden), bf),
            pltpu.VMEM((replicas, frags, frag_rows, cols), bf),
            pltpu.VMEM(frag_global.shape, f32),
            pltpu.VMEM(frag_global.shape, f32),
            pltpu.VMEM(frag_global.shape, f32),
            pltpu.VMEM(frag_global.shape, bf),
            pltpu.VMEM((2, 8, 128), f32),
            pltpu.VMEM((groups, 8, 128), f32),
            pltpu.VMEM((replicas, 8, 128), f32),
            pltpu.VMEM((CAP, width), f32),
            pltpu.VMEM((2, *inputs.shape), bf),
            pltpu.VMEM(inputs.shape, bf),
            dma((6,)),
            dma((7,)),
            dma((2, 2, 3, outer)),
            dma((2, 2, 3, outer)),
            dma((2, outer + 1)),
            dma((2, outer + 1)),
            dma((2, 2, 3, outer)),
            dma((2, 2, 3, outer)),
            dma((2, outer + 1)),
            dma((2, outer + 1)),
            dma((replicas,)),
            dma((replicas,)),
            dma,
            dma((groups,)),
            dma((groups,)),
            dma((replicas,)),
            dma((replicas,)),
            dma((replicas,)),
            dma((replicas,)),
            dma,
        ],
        compiler_params=pltpu.CompilerParams(
            collective_id=0, has_side_effects=True, vmem_limit_bytes=56 * 2**20
        ),
    )(
        inputs,
        routes[0],
        cweights[0],
        grads_in,
        w_gate[0],
        w_up[0],
        w_down[0],
        frag_local[0],
        frag_global,
        frag_moment,
    )
    return (lo[None], gt[None], gg[None], gu[None], gd[None], ng, nm, nl[None])


def body(*operands):
    if lax.axis_size("expert") == SPLIT:
        return pair_body(*operands)
    return general_body(*operands)


def solution(mesh):
    return jax.shard_map(
        body,
        mesh=mesh,
        in_specs=(
            P("replica", "expert", None),
            P("replica", "expert", None),
            P("replica", "expert", None),
            P("replica", None, "expert"),
            P("replica", None, "expert"),
            P("replica", "expert", None),
            P("replica", "expert", None),
            P("replica", None, "expert", None),
            P(None, "expert", "replica"),
            P(None, "expert", "replica"),
        ),
        out_specs=(
            P("replica", "expert", None),
            P("replica", "expert", None),
            P("replica", None, "expert"),
            P("replica", None, "expert"),
            P("replica", "expert", None),
            P(None, "expert", "replica"),
            P(None, "expert", "replica"),
            P("replica", None, "expert", None),
        ),
        check_vma=False,
    )
```

```python
import functools

import jax
import jax.numpy as jnp
from jax import lax
from jax.experimental import pallas as pl
from jax.experimental.pallas import tpu as pltpu
from jax.sharding import PartitionSpec as P

D = 4096
HID = 1024
SPLIT = 8
CAP = 32


OUTER_MOMENTUM = 0.9
OUTER_RATE = 0.7
CLIP_RMS = 0.5


def silu_parts(gate_pre):
    sigmoid_val = jax.nn.sigmoid(gate_pre)
    return (gate_pre * sigmoid_val, sigmoid_val * (1.0 + gate_pre * (1.0 - sigmoid_val)))


def outer_update(pseudo, squares, moment, anchor):
    clip_limit = CLIP_RMS * (HID * D) ** 0.5
    factor = jnp.minimum(jnp.float32(1.0), clip_limit / (jnp.sqrt(squares) + 1e-06))
    clipped = pseudo * factor[:, None, None]
    moment_next = OUTER_MOMENTUM * moment + clipped
    anchor_next = anchor - OUTER_RATE * (OUTER_MOMENTUM * moment_next + clipped)
    return (moment_next, anchor_next)


def general_body(
    tokens, routes, cweights, w_gate, w_up, w_down, grad_out, frag_local, frag_global, frag_moment
):
    groups = lax.axis_size("expert")
    window = groups // SPLIT
    precise = lax.Precision.HIGHEST
    inputs = tokens[0]
    grads_in = grad_out[0]
    route_ids = routes[0]
    weights = cweights[0]
    wg_part = w_gate[0]
    wu_part = w_up[0]
    wd_part = w_down[0]
    model_width = inputs.shape[1]
    experts = jnp.arange(window, dtype=jnp.int32)
    matched = route_ids[:, :, None] == experts[None, None, :]
    routed = jnp.any(matched, axis=1).astype(jnp.int32)
    shares = jnp.sum(jnp.where(matched, weights[:, :, None], jnp.float32(0.0)), axis=1)
    places = jnp.cumsum(routed, axis=0) - 1
    slot_ids = jnp.arange(CAP, dtype=jnp.int32)
    layout = (routed.T[:, None, :] == 1) & (places.T[:, None, :] == slot_ids[None, :, None])
    layout_f = layout.astype(jnp.float32)
    layout_b = layout.astype(jnp.bfloat16)
    combine = layout_f * shares.T[:, None, :]
    slot_share = jnp.sum(combine, axis=2)
    picked = jnp.einsum("ect,td->ecd", layout_b, inputs, preferred_element_type=jnp.float32).astype(
        jnp.bfloat16
    )
    outbound = jnp.broadcast_to(picked[:, None], (window, SPLIT, CAP, model_width)).reshape(
        groups, CAP, model_width
    )
    received = lax.all_to_all(outbound, "expert", split_axis=0, concat_axis=0, tiled=True)
    n_source, n_rows, width_in = received.shape
    flat = received.reshape(n_source * n_rows, width_in)
    gate_pre = jnp.dot(flat, wg_part, preferred_element_type=jnp.float32)
    up_pre = jnp.dot(flat, wu_part, preferred_element_type=jnp.float32)
    silu_val, silu_slope = silu_parts(gate_pre)
    hidden_act = (silu_val * up_pre).astype(jnp.bfloat16)
    partial_value = jnp.dot(hidden_act, wd_part, preferred_element_type=jnp.float32)
    partial_out, hidden_act, gate_pre, up_pre, rows_in = (
        partial_value.reshape(n_source, n_rows, width_in),
        hidden_act.reshape(n_source, n_rows, -1),
        gate_pre.reshape(n_source, n_rows, -1),
        up_pre.reshape(n_source, n_rows, -1),
        received,
    )
    returned = lax.all_to_all(partial_out, "expert", split_axis=0, concat_axis=0, tiled=True)
    expert_out = jnp.sum(returned.reshape(window, SPLIT, CAP, model_width), axis=1)
    layer_out = jnp.einsum(
        "ect,ecd->td", combine, expert_out, precision=precise, preferred_element_type=jnp.float32
    ).astype(jnp.bfloat16)
    dy_picked = jnp.einsum("ect,td->ecd", layout_b, grads_in, preferred_element_type=jnp.float32)
    dy_scaled = (dy_picked * slot_share[:, :, None]).astype(jnp.bfloat16)
    outbound_dy = jnp.broadcast_to(dy_scaled[:, None], (window, SPLIT, CAP, model_width)).reshape(
        groups, CAP, model_width
    )
    rows_dy = lax.all_to_all(outbound_dy, "expert", split_axis=0, concat_axis=0, tiled=True)
    grad_rows = rows_dy.reshape(-1, model_width)
    tok_rows = rows_in.reshape(-1, model_width)
    act_rows = hidden_act.reshape(grad_rows.shape[0], -1)
    gate_rows = gate_pre.reshape(grad_rows.shape[0], -1)
    up_rows = up_pre.reshape(grad_rows.shape[0], -1)
    grad_hidden = jnp.einsum("rd,hd->rh", grad_rows, wd_part, preferred_element_type=jnp.float32)
    silu_val, silu_slope = silu_parts(gate_rows)
    grad_gate_pre = (grad_hidden * up_rows * silu_slope).astype(jnp.bfloat16)
    grad_up_pre = (grad_hidden * silu_val).astype(jnp.bfloat16)
    grad_gate = jnp.einsum(
        "rd,rh->dh", tok_rows, grad_gate_pre, preferred_element_type=jnp.float32
    ).astype(jnp.bfloat16)[None]
    grad_up = jnp.einsum(
        "rd,rh->dh", tok_rows, grad_up_pre, preferred_element_type=jnp.float32
    ).astype(jnp.bfloat16)[None]
    grad_down = jnp.einsum(
        "rh,rd->hd", act_rows, grad_rows, preferred_element_type=jnp.float32
    ).astype(jnp.bfloat16)[None]
    partial_dx = jnp.einsum(
        "rh,dh->rd", grad_gate_pre, wg_part, preferred_element_type=jnp.float32
    ) + jnp.einsum("rh,dh->rd", grad_up_pre, wu_part, preferred_element_type=jnp.float32)
    partial_dx = partial_dx.reshape(groups, CAP, model_width)
    returned_dx = lax.all_to_all(partial_dx, "expert", split_axis=0, concat_axis=0, tiled=True)
    expert_dx = jnp.sum(returned_dx.reshape(window, SPLIT, CAP, model_width), axis=1)
    grad_tokens = jnp.einsum(
        "ect,ecd->td", layout_f, expert_dx, precision=precise, preferred_element_type=jnp.float32
    ).astype(jnp.bfloat16)
    replicas = lax.axis_size("replica")
    local_terms = frag_local[0].astype(jnp.float32)
    summed = lax.psum_scatter(
        local_terms.astype(jnp.bfloat16), "replica", scatter_dimension=2, tiled=True
    ).astype(jnp.float32)
    pseudo = frag_global - summed / replicas
    squares = lax.psum(jnp.sum(pseudo * pseudo, axis=(1, 2)), ("replica", "expert"))
    new_moment, new_global = outer_update(pseudo, squares, frag_moment, frag_global)
    new_local = lax.all_gather(new_global.astype(jnp.bfloat16), "replica", axis=2, tiled=True)[None]
    return (
        layer_out[None],
        grad_tokens[None],
        grad_gate,
        grad_up,
        grad_down,
        new_global,
        new_moment,
        new_local,
    )


MESH = pl.DeviceIdType.MESH
INNER = 2
COLS = 512
SPLITS = ((3584, 2560), (2560, 3584))
NT = (((1,), (1,)), ((), ()))
TN = (((0,), (0,)), ((), ()))


def step_kernel(
    groups,
    replicas,
    splits,
    x_ref,
    routes_ref,
    weights_ref,
    dy_ref,
    wg_ref,
    wu_ref,
    wd_ref,
    fl_ref,
    fg_ref,
    fm_ref,
    lo_ref,
    gt_ref,
    gg_ref,
    gu_ref,
    gd_ref,
    ng_ref,
    nm_ref,
    nl_ref,
    xs,
    ys,
    part,
    part_dx,
    from_pair,
    from_left,
    from_right,
    wgu,
    wd,
    pre,
    hid,
    act_t,
    dpre,
    ggu,
    gdn,
    pieces,
    fg,
    fm,
    pseudo,
    fresh,
    sq_part,
    sq_exp,
    sq_rep,
    total,
    placed,
    grads,
    load_sem,
    store_sem,
    gather_send,
    gather_recv,
    gpair_send,
    gpair_recv,
    red_send,
    red_recv,
    rpair_send,
    rpair_recv,
    frag_send,
    frag_recv,
    frag_own_sem,
    sqe_send,
    sqe_recv,
    sqr_send,
    sqr_recv,
    new_send,
    new_recv,
    new_own_sem,
):
    rep = lax.axis_index("replica")
    me = lax.axis_index("expert")
    outer = groups // INNER
    z = me // INNER
    y = me % INNER
    pair = z * INNER + (1 - y)
    width = x_ref.shape[1]
    hidden = wd_ref.shape[0]
    share_cols = fg_ref.shape[2]
    frags = fg_ref.shape[0]
    frag_rows = fg_ref.shape[1]

    loads = [
        pltpu.make_async_copy(wg_ref, wgu.at[:, pl.ds(0, hidden)], load_sem.at[0]),
        pltpu.make_async_copy(wu_ref, wgu.at[:, pl.ds(hidden, hidden)], load_sem.at[1]),
        pltpu.make_async_copy(wd_ref, wd, load_sem.at[2]),
        pltpu.make_async_copy(fg_ref, fg, load_sem.at[3]),
        pltpu.make_async_copy(fm_ref, fm, load_sem.at[4]),
        pltpu.make_async_copy(dy_ref, grads, load_sem.at[5]),
    ]
    for load in loads:
        load.start()

    barrier = pltpu.get_barrier_semaphore()
    for j in range(1, groups):
        pl.semaphore_signal(
            barrier, inc=1, device_id=(rep, lax.rem(me + j, groups)), device_id_type=MESH
        )
    for j in range(1, replicas):
        pl.semaphore_signal(
            barrier, inc=1, device_id=(lax.rem(rep + j, replicas), me), device_id_type=MESH
        )
    def block(z_of, y_of):
        return pl.ds(pl.multiple_of((z_of * INNER + y_of) * CAP, CAP), CAP)

    def remote(src, dst, send, recv, target):
        return pltpu.make_async_remote_copy(
            src_ref=src,
            dst_ref=dst,
            send_sem=send,
            recv_sem=recv,
            device_id=target,
            device_id_type=MESH,
        )

    def right():
        return (rep, jnp.minimum(z + 1, outer - 1) * INNER + y)

    def left():
        return (rep, jnp.maximum(z - 1, 0) * INNER + y)

    def near(which, gather):
        return pl.ds(0, splits[gather][which])

    def far(which, gather):
        return pl.ds(splits[gather][which], width - splits[gather][which])

    def toward(way):
        return right() if way == 0 else left()

    def other(stream):
        return y if stream == 0 else 1 - y

    def gather_copy(buf, which, way, hop, z_src, stream):
        cols = near(which, 0) if stream == 2 else far(which, 0)
        rows = buf.at[block(z_src, y if stream == 2 else other(stream)), cols]
        return remote(
            rows,
            rows,
            gather_send.at[which, way, stream, hop],
            gather_recv.at[which, way, stream, hop],
            toward(way),
        )

    def gather_pair(buf, which, z_src, y_src):
        rows = buf.at[block(z_src, y_src), near(which, 0)]
        return remote(
            rows, rows, gpair_send.at[which, z_src], gpair_recv.at[which, z_src], (rep, pair)
        )

    def gather_swap(buf, which, y_src):
        rows = buf.at[block(z, y_src), far(which, 0)]
        return remote(
            rows, rows, gpair_send.at[which, outer], gpair_recv.at[which, outer], (rep, pair)
        )

    def gather_both_ways(buf, which, stream):
        @pl.when(z < outer - 1)
        def _():
            gather_copy(buf, which, 0, 0, z, stream).start()

        @pl.when(z > 0)
        def _():
            gather_copy(buf, which, 1, 0, z, stream).start()

    def gather_start(buf, which):
        gather_swap(buf, which, y).start()
        gather_both_ways(buf, which, 2)
        gather_pair(buf, which, z, y).start()
        gather_both_ways(buf, which, 0)

    def gather_turn(buf, which):
        gather_swap(buf, which, 1 - y).wait_recv()
        gather_both_ways(buf, which, 1)

    def gather_step(buf, which, hop):
        for stream in (2, 0, 1):

            @pl.when(z >= hop)
            def _(stream=stream):
                gather_copy(buf, which, 0, hop - 1, z - hop, stream).wait_recv()
                if hop < outer - 1:

                    @pl.when(z < outer - 1)
                    def _():
                        gather_copy(buf, which, 0, hop, z - hop, stream).start()

                if stream == 2:
                    gather_pair(buf, which, z - hop, y).start()

            @pl.when(z + hop < outer)
            def _(stream=stream):
                gather_copy(buf, which, 1, hop - 1, z + hop, stream).wait_recv()
                if hop < outer - 1:

                    @pl.when(z > 0)
                    def _():
                        gather_copy(buf, which, 1, hop, z + hop, stream).start()

                if stream == 2:
                    gather_pair(buf, which, z + hop, y).start()

    def gather_finish(buf, which):
        for z_src in range(outer):
            gather_pair(buf, which, z_src, 1 - y).wait_recv()

    def gather_drain(buf, which):
        for stream in range(3):
            for hop in range(outer - 1):

                @pl.when((z < outer - 1) & (z >= hop))
                def _(stream=stream, hop=hop):
                    gather_copy(buf, which, 0, hop, z - hop, stream).wait_send()

                @pl.when((z > 0) & (z + hop < outer))
                def _(stream=stream, hop=hop):
                    gather_copy(buf, which, 1, hop, z + hop, stream).wait_send()

        for z_src in range(outer):
            gather_pair(buf, which, z_src, y).wait_send()
        gather_swap(buf, which, y).wait_send()

    order = []
    for k in range(outer // 2):
        order += [outer - 1 - k, k]
    if outer % 2:
        order.append(outer // 2)

    def reduce_pair(buf, which, z_dst):
        return remote(
            buf.at[block(z_dst, 1 - y), near(which, 1)],
            from_pair.at[which, z_dst, :, near(which, 1)],
            rpair_send.at[which, z_dst],
            rpair_recv.at[which, z_dst],
            (rep, pair),
        )

    def reduce_swap(buf, which):
        return remote(
            buf.at[block(z, 1 - y), far(which, 1)],
            from_pair.at[which, z, :, far(which, 1)],
            rpair_send.at[which, outer],
            rpair_recv.at[which, outer],
            (rep, pair),
        )

    def landing(which, way, z_dst, stream):
        held = from_left if way == 0 else from_right
        cols = near(which, 1) if stream == 2 else far(which, 1)
        return held.at[which, 1 if stream == 1 else 0, z_dst, :, cols]

    def home(buf, which, z_dst, stream):
        cols = near(which, 1) if stream == 2 else far(which, 1)
        return buf.at[block(z_dst, y if stream == 2 else other(stream)), cols]

    def reduce_line(buf, which, way, z_dst, stream):
        return remote(
            home(buf, which, z_dst, stream),
            landing(which, way, z_dst, stream),
            red_send.at[which, way, stream, z_dst],
            red_recv.at[which, way, stream, z_dst],
            toward(way),
        )

    def reduce_start(buf, which):
        for z_dst in order:
            reduce_pair(buf, which, z_dst).start()

    def add_to(target, *terms):
        value = target[...].astype(jnp.float32)
        for term in terms:
            value = value + term[...].astype(jnp.float32)
        target[...] = value.astype(jnp.bfloat16)

    def reduce_step(buf, which, k, streams=(1, 0, 2)):
        z_dst = order[k]
        for stream in streams:
            pair_term = ()
            if stream == 2:
                reduce_pair(buf, which, z_dst).wait_recv()
                pair_term = (from_pair.at[which, z_dst, :, near(which, 1)],)
            target = home(buf, which, z_dst, stream)
            for way, ahead, behind in (
                (0, z < z_dst, z > 0),
                (1, z > z_dst, z < outer - 1),
            ):

                @pl.when(ahead & behind)
                def _(way=way, stream=stream, target=target, pair_term=pair_term):
                    reduce_line(buf, which, way, z_dst, stream).wait_recv()
                    add_to(target, landing(which, way, z_dst, stream), *pair_term)

                if stream == 2:

                    @pl.when(ahead & jnp.logical_not(behind))
                    def _(target=target, pair_term=pair_term):
                        add_to(target, *pair_term)

                @pl.when(ahead)
                def _(way=way, stream=stream):
                    reduce_line(buf, which, way, z_dst, stream).start()

    def reduce_turn(buf, which):
        target = home(buf, which, z, 1)

        @pl.when(z > 0)
        def _():
            reduce_line(buf, which, 0, z, 1).wait_recv()
            add_to(target, landing(which, 0, z, 1))

        @pl.when(z < outer - 1)
        def _():
            reduce_line(buf, which, 1, z, 1).wait_recv()
            add_to(target, landing(which, 1, z, 1))

        reduce_swap(buf, which).start()

    def reduce_finish(buf, which):
        for stream in (2, 0):
            cols = near(which, 1) if stream == 2 else far(which, 1)
            total[:, cols] = home(buf, which, z, stream)[...].astype(jnp.float32)

            @pl.when(z > 0)
            def _(stream=stream, cols=cols):
                reduce_line(buf, which, 0, z, stream).wait_recv()
                total[:, cols] += landing(which, 0, z, stream)[...].astype(jnp.float32)

            @pl.when(z < outer - 1)
            def _(stream=stream, cols=cols):
                reduce_line(buf, which, 1, z, stream).wait_recv()
                total[:, cols] += landing(which, 1, z, stream)[...].astype(jnp.float32)

        reduce_swap(buf, which).wait_recv()
        total[...] += from_pair[which, z].astype(jnp.float32)

    def reduce_drain(buf, which):
        for z_dst in range(outer):
            reduce_pair(buf, which, z_dst).wait_send()
            for stream in range(3):

                @pl.when(z < z_dst)
                def _(stream=stream, z_dst=z_dst):
                    reduce_line(buf, which, 0, z_dst, stream).wait_send()

                @pl.when(z > z_dst)
                def _(stream=stream, z_dst=z_dst):
                    reduce_line(buf, which, 1, z_dst, stream).wait_send()

        reduce_swap(buf, which).wait_send()

    def columns(index):
        return pl.ds(pl.multiple_of(index * share_cols, share_cols), share_cols)

    def frag_copy(j):
        target = lax.rem(rep + j, replicas)
        return remote(
            fl_ref.at[:, :, columns(target)],
            pieces.at[j],
            frag_send.at[j],
            frag_recv.at[j],
            (target, me),
        )

    def new_copy(j):
        return remote(
            fresh,
            nl_ref.at[:, :, columns(rep)],
            new_send.at[j],
            new_recv.at[j],
            (lax.rem(rep + j, replicas), me),
        )

    def new_arrival(j):
        return remote(
            fresh,
            nl_ref.at[:, :, columns(lax.rem(rep + replicas - j, replicas))],
            new_send.at[j],
            new_recv.at[j],
            (lax.rem(rep + j, replicas), me),
        )

    def sqe_copy(j):
        return remote(
            sq_part.at[0],
            sq_exp.at[j],
            sqe_send.at[j],
            sqe_recv.at[j],
            (rep, lax.rem(me + j, groups)),
        )

    def sqr_copy(j):
        return remote(
            sq_part.at[1],
            sq_rep.at[j],
            sqr_send.at[j],
            sqr_recv.at[j],
            (lax.rem(rep + j, replicas), me),
        )

    tiles = width // COLS

    def tile(index):
        return pl.ds(pl.multiple_of(index * COLS, COLS), COLS)

    count = x_ref.shape[0]
    matched = routes_ref[...] == 0
    flag_row = jnp.broadcast_to(
        jnp.sum(matched.astype(jnp.float32), axis=0, keepdims=True), (CAP, count)
    )
    share_row = jnp.sum(
        jnp.where(matched, weights_ref[...], jnp.float32(0.0)), axis=0, keepdims=True
    )
    before = lax.broadcasted_iota(jnp.int32, (count, count), 0)
    after = lax.broadcasted_iota(jnp.int32, (count, count), 1)
    upper = (before < after).astype(jnp.bfloat16)
    places = jnp.dot(flag_row.astype(jnp.bfloat16), upper, preferred_element_type=jnp.float32)
    slots = lax.broadcasted_iota(jnp.int32, (CAP, count), 0).astype(jnp.float32)
    chosen = (flag_row > 0.5) & (places == slots)
    layout = chosen.astype(jnp.float32).astype(jnp.bfloat16)
    slot_share = jnp.sum(jnp.where(chosen, share_row, 0.0), axis=1, keepdims=True)

    mine = block(z, y)

    @pl.loop(0, tiles)
    def _(t):
        xs[mine, tile(t)] = jnp.dot(
            layout, x_ref[:, tile(t)], preferred_element_type=jnp.float32
        ).astype(jnp.bfloat16)

    pl.semaphore_wait(barrier, groups - 1 + replicas - 1)
    gather_start(xs, 0)
    frag_order = [replicas // 2] + [j for j in range(1, replicas) if j != replicas // 2]
    for j in frag_order:
        frag_copy(j).start()
    own_piece = pltpu.make_async_copy(fl_ref.at[:, :, columns(rep)], pieces.at[0], frag_own_sem)
    own_piece.start()
    loads[5].wait()

    @pl.loop(0, tiles)
    def _(t):
        picked = jnp.dot(layout, grads[:, tile(t)], preferred_element_type=jnp.float32)
        ys[mine, tile(t)] = (picked * slot_share).astype(jnp.bfloat16)

    gather_turn(xs, 0)
    for hop in range(1, outer - 1):
        gather_step(xs, 0, hop)
    gather_start(ys, 1)
    gather_step(xs, 0, outer - 1)
    loads[0].wait()
    loads[1].wait()
    gather_finish(xs, 0)
    gather_turn(ys, 1)

    pre[...] = jnp.zeros_like(pre)

    @pl.loop(0, tiles)
    def _(t):
        pre[...] += jnp.dot(xs[:, tile(t)], wgu[tile(t), :], preferred_element_type=jnp.float32)

    gate_pre = pre[:, :hidden]
    silu_val, _ = silu_parts(gate_pre)
    act = (silu_val * pre[:, hidden:]).astype(jnp.bfloat16)
    hid[...] = act
    act_t[...] = act.astype(jnp.float32).T.astype(jnp.bfloat16)
    loads[2].wait()

    gather_step(ys, 1, 1)
    cut = splits[1][0] // COLS

    def forward(t):
        part[:, tile(t)] = jnp.dot(
            hid[...], wd[:, tile(t)], preferred_element_type=jnp.float32
        ).astype(jnp.bfloat16)

    pl.loop(0, cut)(forward)
    reduce_start(part, 0)
    pl.loop(cut, tiles)(forward)
    reduce_step(part, 0, 0, (1, 0))
    gather_step(ys, 1, 2)
    reduce_step(part, 0, 0, (2,))
    reduce_step(part, 0, 1)
    for hop in range(3, outer):
        gather_step(ys, 1, hop)

    loads[3].wait()
    own_piece.wait()
    for j in range(1, replicas):
        frag_copy(j).wait_recv()
    chunk = 32 if frag_rows % 32 == 0 else 16
    lanes = []
    for f in range(frags):

        def accumulate(i, total, f=f):
            rows = pl.ds(pl.multiple_of(i * chunk, chunk), chunk)
            summed = pieces[0, f, rows, :].astype(jnp.float32)
            for j in range(1, replicas):
                summed += pieces[j, f, rows, :].astype(jnp.float32)
            value = fg[f, rows, :] - summed * (1.0 / replicas)
            pseudo[f, rows, :] = value
            return total + jnp.sum(value * value, axis=0, keepdims=True)

        squared = lax.fori_loop(
            0, frag_rows // chunk, accumulate, jnp.zeros((1, share_cols), jnp.float32)
        )
        lanes.append(jnp.sum(squared, axis=1, keepdims=True))
    row_ids = lax.broadcasted_iota(jnp.int32, (8, 128), 0)
    tile_sum = jnp.zeros((8, 128), jnp.float32)
    for f in range(frags):
        tile_sum = jnp.where(row_ids == f, lanes[f], tile_sum)
    sq_part[0] = tile_sum
    for j in range(1, groups):
        sqe_copy(j).start()

    for k in range(2, outer):
        reduce_step(part, 0, k)
    reduce_turn(part, 0)
    gather_finish(ys, 1)

    for j in range(1, groups):
        sqe_copy(j).wait_recv()
    over_experts = sq_part[0]
    for j in range(1, groups):
        over_experts += sq_exp[j]
    sq_part[1] = over_experts
    for j in range(1, replicas):
        sqr_copy(j).start()

    pre_dact = ggu.at[0]
    pre_dact[...] = jnp.zeros_like(pre_dact)

    @pl.loop(0, tiles)
    def _(t):
        pre_dact[...] += lax.dot_general(
            ys[:, tile(t)], wd[:, tile(t)], NT, preferred_element_type=jnp.float32
        )

    grad_hidden = pre_dact[...]
    silu_val, silu_slope = silu_parts(pre[:, :hidden])
    dpre[:, :hidden] = (grad_hidden * pre[:, hidden:] * silu_slope).astype(jnp.bfloat16)
    dpre[:, hidden:] = (grad_hidden * silu_val).astype(jnp.bfloat16)

    cut_dx = splits[1][1] // COLS

    def backward(t):
        part_dx[:, tile(t)] = lax.dot_general(
            dpre[...], wgu[tile(t), :], NT, preferred_element_type=jnp.float32
        ).astype(jnp.bfloat16)

    pl.loop(0, cut_dx)(backward)
    reduce_start(part_dx, 1)
    pl.loop(cut_dx, tiles)(backward)
    reduce_step(part_dx, 1, 0, (1, 0))

    loads[4].wait()
    for j in range(1, replicas):
        sqr_copy(j).wait_recv()
    squares = sq_part[1]
    for j in range(1, replicas):
        squares += sq_rep[j]
    limit = CLIP_RMS * (HID * D) ** 0.5
    factors = jnp.minimum(jnp.float32(1.0), limit / (jnp.sqrt(squares) + 1e-06))
    for f in range(frags):
        factor = factors[f : f + 1, :1]

        def update(i, carry, f=f, factor=factor):
            rows = pl.ds(pl.multiple_of(i * chunk, chunk), chunk)
            clipped = pseudo[f, rows, :] * factor
            moment = OUTER_MOMENTUM * fm[f, rows, :] + clipped
            anchor = fg[f, rows, :] - OUTER_RATE * (OUTER_MOMENTUM * moment + clipped)
            fm[f, rows, :] = moment
            fg[f, rows, :] = anchor
            fresh[f, rows, :] = anchor.astype(jnp.bfloat16)
            return carry

        lax.fori_loop(0, frag_rows // chunk, update, 0)
    for j in frag_order:
        new_copy(j).start()
    own_new = pltpu.make_async_copy(fresh, nl_ref.at[:, :, columns(rep)], new_own_sem)
    own_new.start()
    stores = [
        pltpu.make_async_copy(fg, ng_ref, store_sem.at[0]),
        pltpu.make_async_copy(fm, nm_ref, store_sem.at[1]),
    ]
    for store in stores:
        store.start()

    def place(which, ref):
        total_b = total[...].astype(jnp.bfloat16)
        for t in range(tiles):
            cols = pl.ds(t * COLS, COLS)
            placed[which, :, cols] = lax.dot_general(
                layout,
                total_b[:, t * COLS : (t + 1) * COLS],
                TN,
                preferred_element_type=jnp.float32,
            ).astype(jnp.bfloat16)
        copy = pltpu.make_async_copy(placed.at[which], ref, store_sem.at[5 + which])
        copy.start()
        return copy

    reduce_step(part_dx, 1, 0, (2,))
    reduce_step(part_dx, 1, 1)
    reduce_finish(part, 0)
    total[...] = total[...] * slot_share
    placed_out = place(0, lo_ref)

    @pl.loop(0, tiles)
    def _(t):
        both = lax.dot_general(
            xs[:, tile(t)], dpre[...], TN, preferred_element_type=jnp.float32
        ).astype(jnp.bfloat16)
        gdn[0, tile(t), :] = both[:, :hidden]
        gdn[1, tile(t), :] = both[:, hidden:]

    more = [
        pltpu.make_async_copy(gdn.at[0], gg_ref, store_sem.at[2]),
        pltpu.make_async_copy(gdn.at[1], gu_ref, store_sem.at[3]),
    ]
    for store in more:
        store.start()
    for k in range(2, outer):
        reduce_step(part_dx, 1, k)
    reduce_turn(part_dx, 1)
    gd_out = wd

    @pl.loop(0, tiles)
    def _(t):
        gd_out[:, tile(t)] = jnp.dot(
            act_t[...], ys[:, tile(t)], preferred_element_type=jnp.float32
        ).astype(jnp.bfloat16)

    last = pltpu.make_async_copy(gd_out, gd_ref, store_sem.at[4])
    last.start()

    reduce_finish(part_dx, 1)
    placed_dx = place(1, gt_ref)

    for buf, which in ((xs, 0), (ys, 1)):
        gather_drain(buf, which)
    for buf, which in ((part, 0), (part_dx, 1)):
        reduce_drain(buf, which)
    for j in range(1, groups):
        sqe_copy(j).wait_send()
    for j in range(1, replicas):
        frag_copy(j).wait_send()
        sqr_copy(j).wait_send()
        new_copy(j).wait_send()
        new_arrival(j).wait_recv()
    own_new.wait()
    for store in stores + more + [last, placed_out, placed_dx]:
        store.wait()


def pair_body(
    tokens, routes, cweights, w_gate, w_up, w_down, grad_out, frag_local, frag_global, frag_moment
):
    groups = lax.axis_size("expert")
    replicas = lax.axis_size("replica")
    inputs, grads_in = tokens[0], grad_out[0]
    width = inputs.shape[1]
    hidden = w_down.shape[1]
    frags, frag_rows, cols = frag_global.shape
    bf, f32 = jnp.bfloat16, jnp.float32
    outer = groups // INNER
    total = groups * CAP
    dma = pltpu.SemaphoreType.DMA
    vmem, hbm = pl.BlockSpec(memory_space=pltpu.VMEM), pl.BlockSpec(memory_space=pl.ANY)
    shape = jax.ShapeDtypeStruct
    lo, gt, gg, gu, gd, ng, nm, nl = pl.pallas_call(
        functools.partial(step_kernel, groups, replicas, SPLITS),
        out_shape=(
            shape(inputs.shape, bf),
            shape(inputs.shape, bf),
            shape((width, hidden), bf),
            shape((width, hidden), bf),
            shape((hidden, width), bf),
            shape(frag_global.shape, f32),
            shape(frag_global.shape, f32),
            shape(frag_local.shape[1:], bf),
        ),
        in_specs=[vmem] * 3 + [hbm] * 7,
        out_specs=(hbm,) * 8,
        scratch_shapes=[
            pltpu.VMEM((total, width), bf),
            pltpu.VMEM((total, width), bf),
            pltpu.VMEM((total, width), bf),
            pltpu.VMEM((total, width), bf),
            pltpu.VMEM((2, outer, CAP, width), bf),
            pltpu.VMEM((2, 2, outer, CAP, width), bf),
            pltpu.VMEM((2, 2, outer, CAP, width), bf),
            pltpu.VMEM((width, 2 * hidden), bf),
            pltpu.VMEM((hidden, width), bf),
            pltpu.VMEM((total, 2 * hidden), f32),
            pltpu.VMEM((total, hidden), bf),
            pltpu.VMEM((hidden, total), bf),
            pltpu.VMEM((total, 2 * hidden), bf),
            pltpu.VMEM((1, total, hidden), f32),
            pltpu.VMEM((2, width, hidden), bf),
            pltpu.VMEM((replicas, frags, frag_rows, cols), bf),
            pltpu.VMEM(frag_global.shape, f32),
            pltpu.VMEM(frag_global.shape, f32),
            pltpu.VMEM(frag_global.shape, f32),
            pltpu.VMEM(frag_global.shape, bf),
            pltpu.VMEM((2, 8, 128), f32),
            pltpu.VMEM((groups, 8, 128), f32),
            pltpu.VMEM((replicas, 8, 128), f32),
            pltpu.VMEM((CAP, width), f32),
            pltpu.VMEM((2, *inputs.shape), bf),
            pltpu.VMEM(inputs.shape, bf),
            dma((6,)),
            dma((7,)),
            dma((2, 2, 3, outer)),
            dma((2, 2, 3, outer)),
            dma((2, outer + 1)),
            dma((2, outer + 1)),
            dma((2, 2, 3, outer)),
            dma((2, 2, 3, outer)),
            dma((2, outer + 1)),
            dma((2, outer + 1)),
            dma((replicas,)),
            dma((replicas,)),
            dma,
            dma((groups,)),
            dma((groups,)),
            dma((replicas,)),
            dma((replicas,)),
            dma((replicas,)),
            dma((replicas,)),
            dma,
        ],
        compiler_params=pltpu.CompilerParams(
            collective_id=0, has_side_effects=True, vmem_limit_bytes=56 * 2**20
        ),
    )(
        inputs,
        routes[0].T,
        cweights[0].T,
        grads_in,
        w_gate[0],
        w_up[0],
        w_down[0],
        frag_local[0],
        frag_global,
        frag_moment,
    )
    return (lo[None], gt[None], gg[None], gu[None], gd[None], ng, nm, nl[None])


def body(*operands):
    if lax.axis_size("expert") == SPLIT:
        return pair_body(*operands)
    return general_body(*operands)


def solution(mesh):
    return jax.shard_map(
        body,
        mesh=mesh,
        in_specs=(
            P("replica", "expert", None),
            P("replica", "expert", None),
            P("replica", "expert", None),
            P("replica", None, "expert"),
            P("replica", None, "expert"),
            P("replica", "expert", None),
            P("replica", "expert", None),
            P("replica", None, "expert", None),
            P(None, "expert", "replica"),
            P(None, "expert", "replica"),
        ),
        out_specs=(
            P("replica", "expert", None),
            P("replica", "expert", None),
            P("replica", None, "expert"),
            P("replica", None, "expert"),
            P("replica", "expert", None),
            P(None, "expert", "replica"),
            P(None, "expert", "replica"),
            P("replica", None, "expert", None),
        ),
        check_vma=False,
    )
```
